256 devices in a mesh: dp: 8 (over x, y_hi), seq: 2 (over core), tensor: 16 (over z, y_lo).
Axes of the slice: x: 4, y: 4 (y_hi: 2, y_lo: 2; y = y_hi * 2 + y_lo), z: 8, core: 2. Of those that a mesh axis runs over, the one named last changes fastest.
Arguments:
- anchor: bfloat16 [8, 384, 8192], P('dp', 'seq'), may hold values from -42 to 42
- augment: bfloat16 [8, 384, 3584], P('dp', 'seq'), may hold values from -6 to 6
- lag: int32 [8], P('dp'), may hold values from 0 to 191
- w_query: bfloat16 [8192, 4096], P(('dp', 'seq'), 'tensor'), may hold values from -0.0625 to 0.0625
- w_key: bfloat16 [3584, 4096], P(('dp', 'seq'), 'tensor'), may hold values from -0.09375 to 0.09375
- w_value: bfloat16 [3584, 4096], P(('dp', 'seq'), 'tensor'), may hold values from -0.09375 to 0.09375
- w_out: bfloat16 [4096, 8192], P('tensor', ('dp', 'seq')), may hold values from -0.375 to 0.375
- cotangent: bfloat16 [8, 384, 8192], P('dp', 'seq', 'tensor'), may hold values from -6 to 6
Outputs:
- update: bfloat16 [8, 384, 8192], P('dp', 'seq', 'tensor')
- grad_query: bfloat16 [8192, 4096], P(('dp', 'seq'), 'tensor')
- grad_key: bfloat16 [3584, 4096], P(('dp', 'seq'), 'tensor')
- grad_value: bfloat16 [3584, 4096], P(('dp', 'seq'), 'tensor')
- grad_out: bfloat16 [4096, 8192], P('tensor', ('dp', 'seq'))
The draws below stay inside these ranges and needn't reach their ends.
All inputs are finite; a program needn't handle non-finite values.
Results may differ from the reference program's by a relative error of at most 0.029.
The reference program's roundings to bfloat16 on the way count: a program that leaves them out, or rounds other values in their place, can miss the bound.
Values may be sent and summed in bfloat16 or wider, within the bound.
A program may use at most 128 MiB of HBM per device.

```python
import jax
import jax.numpy as jnp
from jax import lax

D = 8192
E = 3584
HEADS = 32
HEAD_DIM = 128
TOK_DEV = 192
HD = 4096
HD_DEV = 256
SEQS = 8
LENGTH = 384
N_SEQ = 2
N_TENSOR = 16


def draw_anchor(key, part):
    key = jax.random.fold_in(key, 11)
    base_key = jax.random.fold_in(key, 0)
    extent = (SEQS, LENGTH, D)
    values = jnp.clip(jax.random.normal(base_key, extent, jnp.float32), -6.0, 6.0)
    return values.astype(jnp.bfloat16)


def set_ends(drawn, own_key, smallest, largest):
    longest = drawn.shape.index(max(drawn.shape))
    spots = []
    for shift in (0, 1):
        where = [jax.random.randint(jax.random.fold_in(own_key, axis), (), 0, length) for axis, length in enumerate(drawn.shape)]
        where[longest] = (where[longest] + shift) % drawn.shape[longest]
        spots.append(tuple(where))
    return drawn.at[spots[0]].set(smallest).at[spots[1]].set(largest)


def steps_of(own_key, shape, pieces, least, top_value):
    gain = 1.0
    for dim, blocks in pieces:
        steps = jax.random.uniform(jax.random.fold_in(jax.random.fold_in(own_key, 6), dim), (blocks,), jnp.float32, least / len(pieces), top_value / len(pieces))
        gain = gain * jnp.repeat(jnp.exp(steps), shape[dim] // blocks).reshape((-1,) + (1,) * (len(shape) - 1 - dim))
    return gain


def gaussian(key, dims, scale, bound, cuts=(), held_as=jnp.bfloat16):
    entries = scale * jax.random.normal(key, dims, jnp.float32)
    if cuts:
        entries = entries * steps_of(key, dims, cuts, -0.22, 0.18)
    return jnp.clip(entries, -bound, bound).astype(held_as)


def setup_inputs(seed: int = 0) -> dict:
    key_of = jax.random.split(jax.random.key(seed), 9)
    anchor = draw_anchor(jax.random.fold_in(key_of[8], 71), 0)
    augment = gaussian(key_of[1], (SEQS, LENGTH, E), 1.0, 6.0, ((0, 8), (1, 2)))
    lag = set_ends(jax.random.randint(key_of[2], (SEQS,), 0, TOK_DEV), jax.random.fold_in(key_of[2], 1), 0, TOK_DEV - 1).astype(jnp.int32)
    w_query = gaussian(key_of[3], (D, HD), D ** -0.5, 0.0625, ((0, 16), (1, 16)))
    w_key = gaussian(key_of[4], (E, HD), E ** -0.5, 0.09375, ((0, 16), (1, 16)))
    w_value = gaussian(key_of[5], (E, HD), E ** -0.5, 0.09375, ((0, 16), (1, 16)))
    w_out = gaussian(key_of[6], (HD, D), (HD // 16) ** -0.5, 0.375, ((0, 16), (1, 16)))
    cotangent = gaussian(key_of[7], (SEQS, LENGTH, D), 1.0, 6.0, ((0, 8), (1, 2), (2, 16)))
    return {"anchor": anchor, "augment": augment, "lag": lag, "w_query": w_query, "w_key": w_key, "w_value": w_value, "w_out": w_out, "cotangent": cotangent}


def attend(query_head, key_head, lag_one):
    position = jnp.arange(LENGTH, dtype=jnp.int32)
    allowed = position[None, :] <= position[:, None] + lag_one
    scores = jnp.dot(query_head, key_head.T, preferred_element_type=jnp.float32) * (HEAD_DIM ** -0.5)
    scores = jnp.where(allowed, scores, -jnp.inf)
    highest = jnp.max(scores, axis=1, keepdims=True)
    expo = jnp.exp(scores - highest)
    return expo / jnp.sum(expo, axis=1, keepdims=True)


def block_sum(left, right):
    left_blocks = left.reshape(N_SEQ, TOK_DEV, left.shape[1]).astype(jnp.float32)
    right_blocks = right.reshape(N_SEQ, TOK_DEV, right.shape[1]).astype(jnp.float32)
    partial_terms = jnp.einsum("nta,ntb->nab", left_blocks, right_blocks)
    partial_terms = lax.optimization_barrier(partial_terms.astype(jnp.bfloat16))
    return jnp.sum(partial_terms.astype(jnp.float32), axis=0)


def split_heads(matrix):
    return matrix.reshape(LENGTH, HEADS, HEAD_DIM).transpose(1, 0, 2)


def join_heads(stacked):
    return stacked.transpose(1, 0, 2).reshape(LENGTH, HD)


def reference(anchor, augment, lag, w_query, w_key, w_value, w_out, cotangent):
    def one_sequence(carry, inputs):
        anchor_one, augment_one, lag_one, cotangent_one = inputs
        query = jnp.dot(anchor_one, w_query, preferred_element_type=jnp.float32).astype(jnp.bfloat16)
        keys = jnp.dot(augment_one, w_key, preferred_element_type=jnp.float32).astype(jnp.bfloat16)
        values = jnp.dot(augment_one, w_value, preferred_element_type=jnp.float32).astype(jnp.bfloat16)
        query_heads = split_heads(query)
        key_heads = split_heads(keys)
        value_heads = split_heads(values)

        def forward_head(parts):
            query_head, key_head, value_head = parts
            probs = attend(query_head, key_head, lag_one)
            return jnp.dot(probs.astype(jnp.bfloat16), value_head, preferred_element_type=jnp.float32).astype(jnp.bfloat16)

        context_heads = lax.map(forward_head, (query_heads, key_heads, value_heads))
        context = join_heads(context_heads)
        context_blocks = context.reshape(LENGTH, N_TENSOR, HD_DEV).transpose(1, 0, 2)
        out_blocks = w_out.reshape(N_TENSOR, HD_DEV, D)

        def add_block(total, pair):
            part_term = jnp.dot(pair[0], pair[1], preferred_element_type=jnp.float32)
            part_term = lax.optimization_barrier(part_term.astype(jnp.bfloat16))
            return total + part_term.astype(jnp.float32), None

        summed, _ = lax.scan(add_block, jnp.zeros((LENGTH, D), jnp.float32), (context_blocks, out_blocks))
        update_one = summed.astype(jnp.bfloat16)
        back_context = jnp.dot(cotangent_one, w_out.T, preferred_element_type=jnp.float32).astype(jnp.bfloat16)
        back_heads = split_heads(back_context)

        def backward_head(parts):
            query_head, key_head, value_head, context_head, back_head = parts
            probs = attend(query_head, key_head, lag_one)
            attention = probs.astype(jnp.bfloat16)
            dprobs = jnp.dot(back_head, value_head.T, preferred_element_type=jnp.float32)
            delta = jnp.sum(back_head.astype(jnp.float32) * context_head.astype(jnp.float32), axis=1, keepdims=True)
            dscores = (probs * (dprobs - delta) * (HEAD_DIM ** -0.5)).astype(jnp.bfloat16)
            query_back = jnp.dot(dscores, key_head, preferred_element_type=jnp.float32).astype(jnp.bfloat16)
            key_back = jnp.dot(dscores.T, query_head, preferred_element_type=jnp.float32).astype(jnp.bfloat16)
            value_back = jnp.dot(attention.T, back_head, preferred_element_type=jnp.float32).astype(jnp.bfloat16)
            return query_back, key_back, value_back

        query_back, key_back, value_back = lax.map(backward_head, (query_heads, key_heads, value_heads, context_heads, back_heads))
        grad_q, grad_k, grad_v, grad_o = carry
        grad_q = grad_q + block_sum(anchor_one, join_heads(query_back))
        grad_k = grad_k + block_sum(augment_one, join_heads(key_back))
        grad_v = grad_v + block_sum(augment_one, join_heads(value_back))
        grad_o = grad_o + block_sum(context, cotangent_one)
        return (grad_q, grad_k, grad_v, grad_o), update_one

    start_carry = (jnp.zeros((D, HD), jnp.float32), jnp.zeros((E, HD), jnp.float32),
                   jnp.zeros((E, HD), jnp.float32), jnp.zeros((HD, D), jnp.float32))
    totals, update = lax.scan(one_sequence, start_carry, (anchor, augment, lag, cotangent))
    return (update, totals[0].astype(jnp.bfloat16), totals[1].astype(jnp.bfloat16),
            totals[2].astype(jnp.bfloat16), totals[3].astype(jnp.bfloat16))
```

```python
import functools

import jax
import jax.numpy as jnp
from jax import lax
from jax.experimental import pallas as pl
from jax.experimental.pallas import tpu as pltpu
from jax.sharding import PartitionSpec as P

MESH = pl.DeviceIdType.MESH
BF = jnp.bfloat16
F32 = jnp.float32
HEAD = 128
TOK = 192
LEN = 384
NS = 8
COPIES = 128


def nn(a, b):
    return jnp.dot(a, b, preferred_element_type=F32)


def nt(a, b):
    return lax.dot_general(a, b, (((1,), (1,)), ((), ())), preferred_element_type=F32)


def tn(a, b):
    return lax.dot_general(a, b, (((0,), (0,)), ((), ())), preferred_element_type=F32)


def kernel(
    anchor, augment, lag, w_query, w_key, w_value, w_out, cot_in,
    update, g_query, g_key, g_value, g_out,
    anc, anc_t, sts, sts_t, cot, wq, wkv, wo,
    s_out, s_kv, s_q, upd, rz, ru,
    ra_out, rc_out, ry_out, ra_kv, rc_kv, ry_kv, ra_q, rc_q, ry_q,
    part, part_kv, other, other_kv, q_h, k_h, v_h, b_h, probs, att, ctx, qb, kvb,
    send, recv, near_send, near_recv, fin_recv, local,
):
    dp, c, t = lax.axis_index("dp"), lax.axis_index("seq"), lax.axis_index("tensor")
    z, yl = t // 2, t % 2
    o = 1 - c
    xr, xl = (dp + 2) % NS, (dp + 6) % NS
    yp = dp + 1 - 2 * (dp % 2)
    tn_ = t + 1 - 2 * yl
    to_xr, to_xl, to_yp = (xr, c, t), (xl, c, t), (yp, c, t)
    to_zr, to_zl = (dp, c, (t + 2) % 16), (dp, c, (t + 14) % 16)
    to_sib = (dp, o, t)
    same = c == yl

    barrier = pltpu.get_barrier_semaphore()
    partners = (to_xr, to_xl, to_yp, to_zr, to_zl, to_sib, (dp, 0, tn_), (dp, 1, tn_))
    for who in partners:
        pl.semaphore_signal(barrier, inc=1, device_id=who, device_id_type=MESH)
    pl.semaphore_wait(barrier, len(partners))

    started = []

    def push(src, dst, who):
        i = len(started)
        copy = pltpu.make_async_remote_copy(
            src_ref=src, dst_ref=dst, send_sem=send.at[i], recv_sem=recv.at[i],
            device_id=who, device_id_type=MESH,
        )
        copy.start()
        started.append(copy)
        return copy

    locals_ = []

    def fetch(src, dst):
        copy = pltpu.make_async_copy(src, dst, local.at[len(locals_)])
        copy.start()
        locals_.append(copy)
        return copy

    def col(i, n):
        return pl.ds(pl.multiple_of(i * n, n), n)

    mine = pl.ds(pl.multiple_of(c * TOK, TOK), TOK)
    head = col(c, HEAD)
    head_o = col(o, HEAD)

    def kv_rows(k, half):
        base = (2 * k + c) * 224
        if half is None:
            return pl.ds(pl.multiple_of(base, 224), 224)
        return pl.ds(pl.multiple_of(base + half * 112, 112), 112)

    def slot_k(k, half=None):
        return wkv.at[kv_rows(k, half), pl.ds(0, 256)]

    def slot_v(k, half=None):
        return wkv.at[kv_rows(k, half), pl.ds(256, 256)]

    def slot_q(k, half=None):
        return wq.at[k] if half is None else wq.at[k, pl.ds(half * 256, 256)]

    def slot_o(k, half=None):
        return wo.at[k] if half is None else wo.at[k, pl.ds(half * 128, 128)]

    def flip(k):
        return k + 1 - 2 * (k % 2)

    class YFirst:
        def __init__(self, src, slot):
            self.slot = slot
            self.own = [push(src, slot(dp), w) for w in (to_xr, to_xl, to_yp)]
            fetch(src, slot(dp))

        def from_y(self):
            self.own[2].wait_recv()
            s = self.slot(yp)
            self.far = [push(s, s, to_xr), push(s, s, to_xl)]

        def from_x(self):
            self.own[0].wait_recv()
            self.own[1].wait_recv()
            a, b = self.slot(xl, 0), self.slot(xr, 1)
            self.halves = [push(a, a, to_xr), push(b, b, to_xl)]

        def from_x_far(self):
            self.far[0].wait_recv()
            self.far[1].wait_recv()
            a, b = self.slot(flip(xl), 0), self.slot(flip(xr), 1)
            self.halves += [push(a, a, to_xr), push(b, b, to_xl)]

        def finish(self):
            for copy in self.halves:
                copy.wait_recv()

    class XFirst:
        def __init__(self, src, slot):
            self.slot = slot
            self.own = [push(src, slot(dp), w) for w in (to_yp, to_xr, to_xl)]
            fetch(src, slot(dp))

        def from_x(self):
            self.own[1].wait_recv()
            self.own[2].wait_recv()
            a, b = self.slot(xl, 0), self.slot(xr, 1)
            self.halves = [push(a, a, to_xr), push(b, b, to_xl)]
            a, b = self.slot(xl), self.slot(xr)
            self.last = [self.own[0], push(a, a, to_yp), push(b, b, to_yp)]

        def from_x_far(self):
            far = (dp + 4) % NS
            for half in (0, 1):
                self.halves[half].wait_recv()
                s = self.slot(far, half)
                self.last.append(push(s, s, to_yp))

        def finish(self):
            for copy in self.last:
                copy.wait_recv()

    ag_k = YFirst(w_key, slot_k)
    ag_v = YFirst(w_value, slot_v)

    cot_dst = cot.at[z, mine]
    cot_far = pltpu.make_async_remote_copy(
        src_ref=cot_in.at[0], dst_ref=cot_dst, send_sem=near_send.at[0], recv_sem=near_recv.at[c],
        device_id=(dp, yl, tn_), device_id_type=MESH)
    cot_sib = pltpu.make_async_remote_copy(
        src_ref=cot_in.at[0], dst_ref=cot_dst, send_sem=near_send.at[1], recv_sem=near_recv.at[c],
        device_id=to_sib, device_id_type=MESH)
    cot_own = pltpu.make_async_copy(cot_in.at[0], cot_dst, near_recv.at[c])
    cot_far.start()

    @pl.when(same)
    def _():
        cot_own.start()

    @pl.when(jnp.logical_not(same))
    def _():
        cot_sib.start()

    ag_q = YFirst(w_query, slot_q)
    ag_o = XFirst(w_out, slot_o)

    sib = [push(augment.at[0], sts.at[mine], to_sib)]
    fetch(augment.at[0], sts.at[mine])
    for k in range(NS):
        sib.append(push(anchor.at[0, :, pl.ds(pl.multiple_of((2 * k + o) * 512, 512), 512)], anc.at[k, mine], to_sib))
        fetch(anchor.at[0, :, pl.ds(pl.multiple_of((2 * k + c) * 512, 512), 512)], anc.at[k, mine])

    zero = jnp.zeros((224, 512), BF)
    for k in range(NS):
        wkv[pl.ds(pl.multiple_of((2 * k + o) * 224, 224), 224), :] = zero

    for h in (0, 1):
        pltpu.make_async_copy(cot.at[z, pl.ds(h * TOK, TOK)], cot.at[z, pl.ds(h * TOK, TOK)], near_recv.at[h]).wait()
    ring = []

    def ring_step(s):
        if s > 1:
            for copy in ring[-1]:
                copy.wait_recv()
        if s < 4:
            a, b = cot.at[(z + 9 - s) % NS], cot.at[(z + s - 1) % NS]
        else:
            a, b = cot.at[(z + 5) % NS, pl.ds(0, TOK)], cot.at[(z + 3) % NS, pl.ds(TOK, TOK)]
        ring.append([push(a, a, to_zr), push(b, b, to_zl)])

    ring_step(1)
    ag_k.from_y()
    ag_k.from_x()
    ag_v.from_y()
    ag_v.from_x()

    for copy in sib:
        copy.wait_recv()
    for copy in locals_:
        copy.wait()

    def turn_sts(j, _):
        sts_t[col(j, 512), :] = sts[:, col(j, 512)].T
        return _

    def turn_anc(k, _):
        anc_t[k] = anc[k].T
        return _

    lax.fori_loop(0, 7, turn_sts, 0)
    ring_step(2)
    ag_q.from_y()
    ag_q.from_x()
    lax.fori_loop(0, NS, turn_anc, 0)
    ag_o.from_x()
    ring_step(3)
    ag_k.from_x_far()
    ag_v.from_x_far()
    ag_q.from_x_far()
    ag_o.from_x_far()
    ag_k.finish()
    ag_v.finish()
    ring_step(4)

    part_kv[...] = nn(sts[:, pl.ds(0, 512)], wkv[pl.ds(0, 512), :])

    def add_kv(j, _):
        part_kv[...] += nn(sts[:, col(j, 512)], wkv[col(j, 512), :])
        return _

    lax.fori_loop(1, 7, add_kv, 0)
    ex_k = push(part_kv.at[:, head_o], other_kv.at[0], to_sib)
    ex_v = push(part_kv.at[:, pl.ds(pl.multiple_of(256 + o * HEAD, HEAD), HEAD)], other_kv.at[1], to_sib)
    ag_q.finish()
    part[0] = nn(anc[0], wq[0])

    def add_q(k, _):
        part[0] += nn(anc[k], wq[k])
        return _

    lax.fori_loop(1, NS, add_q, 0)
    ex_q = push(part.at[0, :, head_o], other.at[0], to_sib)
    ex_k.wait_recv()
    k_h[...] = (part_kv[:, head] + other_kv[0]).astype(BF)
    ex_v.wait_recv()
    v_h[...] = (part_kv[:, pl.ds(pl.multiple_of(256 + c * HEAD, HEAD), HEAD)] + other_kv[1]).astype(BF)
    ex_q.wait_recv()
    q_h[...] = (part[0, :, head] + other[0]).astype(BF)

    factor = HEAD ** (-0.5)
    step = 128
    for r in range(LEN // step):
        rows = pl.ds(r * step, step)
        scores = nt(q_h[rows, :], k_h[...]) * factor
        reach = lax.broadcasted_iota(jnp.int32, (step, LEN), 0) + (r * step + lag[0])
        allowed = lax.broadcasted_iota(jnp.int32, (step, LEN), 1) <= reach
        scores = jnp.where(allowed, scores, -jnp.inf)
        expo = jnp.exp(scores - jnp.max(scores, axis=1, keepdims=True))
        p = expo / jnp.sum(expo, axis=1, keepdims=True)
        probs[rows, :] = p
        a = p.astype(BF)
        att[rows, :] = a
        ctx[rows, head] = nn(a, v_h[...]).astype(BF)
    ex_ctx = push(ctx.at[:, head], ctx.at[:, head], to_sib)

    ag_o.finish()
    for copy in ring[-1]:
        copy.wait_recv()
    part[1] = nt(cot[0], wo[0])

    def add_b(k, _):
        part[1] += nt(cot[k], wo[k])
        return _

    lax.fori_loop(1, NS, add_b, 0)
    ex_b = push(part.at[1, :, head_o], other.at[1], to_sib)
    ex_ctx.wait_recv()

    def slot(off, j):
        k = (dp + 2 * off + NS) % NS
        return flip(k) if j else k

    class XFirstSum:
        def __init__(self, s, ra, rc, ry, make, out):
            self.s, self.ra, self.rc, self.ry, self.out = s, ra, rc, ry, out
            n = s.shape[1] // 2
            self.lo, self.hi = pl.ds(0, n), pl.ds(n, n)
            lo, hi = self.lo, self.hi
            self.a, self.b = [], []
            for j in (0, 1):
                k = slot(2, j)
                make(k)
                self.a += [push(s.at[k, lo], ra.at[0, j], to_xr), push(s.at[k, hi], ra.at[1, j], to_xl)]
            for j in (0, 1):
                k, m = slot(1, j), slot(-1, j)
                make(k)
                self.b.append(push(s.at[k, hi], rc.at[0, j, hi], to_xr))
                make(m)
                self.b.append(push(s.at[m, lo], rc.at[1, j, lo], to_xl))
            for j in (1, 0):
                make(slot(0, j))

        def pass_on(self):
            s, ra, rc = self.s, self.ra, self.rc
            for j in (0, 1):
                k, m = slot(1, j), slot(-1, j)
                self.a[2 * j].wait_recv()
                s[k, self.lo] = (s[k, self.lo].astype(F32) + ra[0, j].astype(F32)).astype(BF)
                self.b.append(push(s.at[k, self.lo], rc.at[0, j, self.lo], to_xr))
                self.a[2 * j + 1].wait_recv()
                s[m, self.hi] = (s[m, self.hi].astype(F32) + ra[1, j].astype(F32)).astype(BF)
                self.b.append(push(s.at[m, self.hi], rc.at[1, j, self.hi], to_xl))

        def total(self, j):
            k = slot(0, j)
            return self.s[k].astype(F32) + self.rc[0, j].astype(F32) + self.rc[1, j].astype(F32)

        def across(self):
            for copy in self.b:
                copy.wait_recv()
            k = slot(0, 1)
            self.s[k] = self.total(1).astype(BF)
            self.y = push(self.s.at[k], self.ry, to_yp)

        def finish(self):
            self.y.wait_recv()
            self.out(self.total(0) + self.ry[...].astype(F32))

    class YFirstSum:
        def __init__(self, s, ra, rc, ry, make, out):
            self.s, self.ra, self.rc, self.ry, self.out = s, ra, rc, ry, out
            n = s.shape[1] // 2
            self.lo, self.hi = pl.ds(0, n), pl.ds(n, n)
            self.y = []
            for i, off in enumerate((2, 1, -1, 0)):
                k = slot(off, 1)
                make(k)
                self.y.append(push(s.at[k], ry.at[i], to_yp))
            for off in (2, 1, -1, 0):
                make(slot(off, 0))

        def add(self, k, rows, got):
            self.s[k, rows] = (self.s[k, rows].astype(F32) + got.astype(F32)).astype(BF)

        def from_y(self):
            s, ra, rc, ry, lo, hi = self.s, self.ra, self.rc, self.ry, self.lo, self.hi
            self.y[0].wait_recv()
            k = slot(2, 0)
            s[k] = (s[k].astype(F32) + ry[0].astype(F32)).astype(BF)
            self.a = [push(s.at[k, lo], ra.at[0], to_xr), push(s.at[k, hi], ra.at[1], to_xl)]

        def from_y_near(self):
            s, rc, ry, lo, hi = self.s, self.rc, self.ry, self.lo, self.hi
            k, m = slot(1, 0), slot(-1, 0)
            self.y[1].wait_recv()
            s[k] = (s[k].astype(F32) + ry[1].astype(F32)).astype(BF)
            self.b = [push(s.at[k, hi], rc.at[0, hi], to_xr)]
            self.y[2].wait_recv()
            s[m] = (s[m].astype(F32) + ry[2].astype(F32)).astype(BF)
            self.b.append(push(s.at[m, lo], rc.at[1, lo], to_xl))

        def pass_on(self):
            k, m = slot(1, 0), slot(-1, 0)
            self.a[0].wait_recv()
            self.add(k, self.lo, self.ra[0])
            self.b.append(push(self.s.at[k, self.lo], self.rc.at[0, self.lo], to_xr))
            self.a[1].wait_recv()
            self.add(m, self.hi, self.ra[1])
            self.b.append(push(self.s.at[m, self.hi], self.rc.at[1, self.hi], to_xl))

        def finish(self):
            self.y[3].wait_recv()
            for copy in self.b:
                copy.wait_recv()
            k = slot(0, 0)
            self.out(self.s[k].astype(F32) + self.ry[3].astype(F32)
                     + self.rc[0].astype(F32) + self.rc[1].astype(F32))

    def make_out(k):
        s_out[k] = tn(ctx[...], cot[k]).astype(BF)

    def put_out(total):
        g_out[...] = total.astype(BF)

    rs_out = XFirstSum(s_out, ra_out, rc_out, ry_out, make_out, put_out)

    def make_upd(k, _):
        upd[k] = nn(ctx[...], wo[k]).astype(BF)
        return _

    lax.fori_loop(0, NS, make_upd, 0)
    zsum = []

    def z_step(s):
        if s == 1:
            far = (z + 4) % NS
            a, b = upd.at[far, pl.ds(0, TOK)], upd.at[far, pl.ds(TOK, TOK)]
            da, db = rz.at[0, 0, pl.ds(0, TOK)], rz.at[1, 0, pl.ds(TOK, TOK)]
        else:
            for copy in zsum[-1]:
                copy.wait_recv()
            k, m = (z + 5 - s) % NS, (z + 3 + s) % NS
            rows_k, rows_m = (pl.ds(0, TOK), pl.ds(TOK, TOK)) if s == 2 else (pl.ds(0, LEN), pl.ds(0, LEN))
            upd[k, rows_k] = (upd[k, rows_k].astype(F32) + rz[0, s - 2, rows_k].astype(F32)).astype(BF)
            upd[m, rows_m] = (upd[m, rows_m].astype(F32) + rz[1, s - 2, rows_m].astype(F32)).astype(BF)
            a, b = upd.at[k], upd.at[m]
            da, db = rz.at[0, s - 1], rz.at[1, s - 1]
        zsum.append([push(a, da, to_zr), push(b, db, to_zl)])

    z_step(1)

    ex_b.wait_recv()
    b_h[...] = (part[1, :, head] + other[1]).astype(BF)
    for r in range(LEN // step):
        rows = pl.ds(r * step, step)
        dprobs = nt(b_h[rows, :], v_h[...])
        delta = jnp.sum(b_h[rows, :].astype(F32) * ctx[rows, head].astype(F32), axis=1, keepdims=True)
        ds = (probs[rows, :] * (dprobs - delta) * factor).astype(BF)
        qb[rows, head] = nn(ds, k_h[...]).astype(BF)
        kt = tn(ds, q_h[rows, :])
        vt = tn(att[rows, :], b_h[rows, :])
        if r == 0:
            other_kv[0] = kt
            other_kv[1] = vt
        else:
            other_kv[0] += kt
            other_kv[1] += vt
    head_v = pl.ds(pl.multiple_of(256 + c * HEAD, HEAD), HEAD)
    kvb[:, head] = other_kv[0].astype(BF)
    kvb[:, head_v] = other_kv[1].astype(BF)
    ex_kb = push(kvb.at[:, head], kvb.at[:, head], to_sib)
    ex_vb = push(kvb.at[:, head_v], kvb.at[:, head_v], to_sib)
    ex_qb = push(qb.at[:, head], qb.at[:, head], to_sib)
    rs_out.pass_on()
    z_step(2)

    def make_kv(k):
        s_kv[k] = nn(sts_t[pl.ds(pl.multiple_of((2 * k + c) * 224, 224), 224), :], kvb[...]).astype(BF)

    def put_kv(total):
        g_key[...] = total[:, :256].astype(BF)
        g_value[...] = total[:, 256:].astype(BF)

    def make_q(k):
        s_q[k] = nn(anc_t[k], qb[...]).astype(BF)

    def put_q(total):
        g_query[...] = total.astype(BF)

    ex_qb.wait_recv()
    rs_q = YFirstSum(s_q, ra_q, rc_q, ry_q, make_q, put_q)
    ex_kb.wait_recv()
    ex_vb.wait_recv()
    rs_kv = XFirstSum(s_kv, ra_kv, rc_kv, ry_kv, make_kv, put_kv)

    rs_q.from_y()
    z_step(3)
    rs_out.across()
    rs_q.from_y_near()
    rs_kv.pass_on()
    z_step(4)
    rs_q.pass_on()
    rs_kv.across()
    rs_out.finish()

    for copy in zsum[-1]:
        copy.wait_recv()
    upd[z] = (upd[z].astype(F32) + rz[0, 3].astype(F32) + rz[1, 3].astype(F32)).astype(BF)
    kept = upd.at[z, mine]
    given = upd.at[z, pl.ds(pl.multiple_of(o * TOK, TOK), TOK)]
    fin_own = pltpu.make_async_copy(kept, ru.at[0], fin_recv.at[0])
    fin_sib = pltpu.make_async_remote_copy(
        src_ref=given, dst_ref=ru.at[0], send_sem=near_send.at[2], recv_sem=fin_recv.at[0],
        device_id=to_sib, device_id_type=MESH)
    fin_far = [
        pltpu.make_async_remote_copy(
            src_ref=upd.at[z, pl.ds(h * TOK, TOK)], dst_ref=ru.at[1], send_sem=near_send.at[3 + h],
            recv_sem=fin_recv.at[1], device_id=(dp, h, tn_), device_id_type=MESH)
        for h in (0, 1)
    ]

    @pl.when(same)
    def _():
        fin_own.start()
        fin_sib.start()

    @pl.when(jnp.logical_not(same))
    def _():
        fin_far[0].start()
        fin_far[1].start()

    rs_kv.finish()
    rs_q.finish()
    for i in (0, 1):
        pltpu.make_async_copy(ru.at[i], ru.at[i], fin_recv.at[i]).wait()
    update[0] = (ru[0].astype(F32) + ru[1].astype(F32)).astype(BF)

    for copy in started:
        copy.wait_send()
    cot_far.wait_send()

    @pl.when(jnp.logical_not(same))
    def _():
        cot_sib.wait_send()
        fin_far[0].wait_send()
        fin_far[1].wait_send()

    @pl.when(same)
    def _():
        fin_sib.wait_send()


def local(*args):
    vm = pltpu.VMEM
    shapes = [
        ((1, TOK, 512), BF), ((512, 256), BF), ((224, 256), BF), ((224, 256), BF), ((256, 512), BF),
    ]
    scratch = [
        vm((NS, LEN, 512), BF), vm((NS, 512, LEN), BF), vm((LEN, 3584), BF), vm((3584, LEN), BF),
        vm((NS, LEN, 512), BF), vm((NS, 512, 256), BF), vm((3584, 512), BF), vm((NS, 256, 512), BF),
        vm((NS, 256, 512), BF), vm((NS, 224, 512), BF), vm((NS, 512, 256), BF),
        vm((NS, LEN, 512), BF), vm((2, 4, LEN, 512), BF), vm((2, TOK, 512), BF),
        vm((2, 2, 128, 512), BF), vm((2, 2, 256, 512), BF), vm((256, 512), BF),
        vm((2, 2, 112, 512), BF), vm((2, 2, 224, 512), BF), vm((224, 512), BF),
        vm((2, 256, 256), BF), vm((2, 512, 256), BF), vm((4, 512, 256), BF),
        vm((2, LEN, 256), F32), vm((LEN, 512), F32), vm((2, LEN, HEAD), F32), vm((2, LEN, HEAD), F32),
        vm((LEN, HEAD), BF), vm((LEN, HEAD), BF), vm((LEN, HEAD), BF), vm((LEN, HEAD), BF),
        vm((LEN, LEN), F32), vm((LEN, LEN), BF), vm((LEN, 256), BF), vm((LEN, 256), BF), vm((LEN, 512), BF),
        pltpu.SemaphoreType.DMA((COPIES,)), pltpu.SemaphoreType.DMA((COPIES,)),
        pltpu.SemaphoreType.DMA((5,)), pltpu.SemaphoreType.DMA((2,)), pltpu.SemaphoreType.DMA((2,)),
        pltpu.SemaphoreType.DMA((16,)),
    ]
    any_ = pl.BlockSpec(memory_space=pl.ANY)
    return pl.pallas_call(
        kernel,
        out_shape=[jax.ShapeDtypeStruct(s, d) for s, d in shapes],
        in_specs=[any_, any_, pl.BlockSpec(memory_space=pltpu.SMEM)] + [any_] * 5,
        out_specs=[pl.BlockSpec(memory_space=pltpu.VMEM)] * 5,
        scratch_shapes=scratch,
        compiler_params=pltpu.CompilerParams(
            collective_id=0, has_side_effects=True, vmem_limit_bytes=58 * 2**20
        ),
        name="block",
    )(*args)


def solution(mesh):
    placed = (
        P("dp", "seq", None),
        P("dp", "seq", None),
        P("dp"),
        P(("dp", "seq"), "tensor"),
        P(("dp", "seq"), "tensor"),
        P(("dp", "seq"), "tensor"),
        P("tensor", ("dp", "seq")),
        P("dp", "seq", "tensor"),
    )
    return jax.shard_map(
        local,
        mesh=mesh,
        in_specs=placed,
        out_specs=(
            P("dp", "seq", "tensor"),
            P(("dp", "seq"), "tensor"),
            P(("dp", "seq"), "tensor"),
            P(("dp", "seq"), "tensor"),
            P("tensor", ("dp", "seq")),
        ),
        check_vma=False,
    )
```

```python
import jax
import jax.numpy as jnp
from jax import lax
from jax.experimental import pallas as pl
from jax.experimental.pallas import tpu as pltpu
from jax.sharding import PartitionSpec as P

MESH = pl.DeviceIdType.MESH
BF = jnp.bfloat16
F32 = jnp.float32
HEAD = 128
TOK = 192
LEN = 384
NS = 8
COPIES = 256

Q_Y, O_Y, GQ_Y, GO_Y = 384, 128, 320, 128

ORDER = (
    "z1a", "z1b", "kv.fx", "kv.fy", "qA.fx", "qB.fx", "z2a", "turn0", "turn1", "turn2", "turn3", "turn4",
    "qB.fy", "turn5", "z2b", "turn6", "turn7", "kv.fxf", "z3a", "qA.fxf", "own_o", "qB.fxf", "z3b", "kv",
    "oA.fx", "z4a", "oB.fx", "q", "oA.fxf", "oB.fy", "attn0", "attn1", "attn2", "oB.fxf", "goA.y0", "goA.y1",
    "goA.y2", "goA.y3", "goB.a0", "goB.a1", "goB.b0", "goB.b1", "goA.m", "goB.m0", "bc", "upd", "goB.p0",
    "goA.a", "goB.p1", "bwd0", "bwd1", "goA.b", "bwd2", "u2a", "goA.b_", "goA.p", "goA.p_", "goB.y", "gkv.a0",
    "gkv.a1", "gkv.b0", "gkv.b1", "u3b", "gqA.y0", "gqA.y1", "gqA.y2", "gqA.y3", "gqB.a0", "gqB.a1", "gqB.b0",
    "gqB.b1", "goA.f", "gkv.m0", "goB.f", "gqA.m", "gqB.m0", "gkv.p0", "u3a", "gkv.p1", "gqA.a", "u4b",
    "gqA.b", "gqB.p0", "u4a", "gqB.p1", "gqA.b_", "gkv.y", "u5", "gqA.p", "gqA.p_", "gqB.y", "gqA.f", "gkv.f",
    "ufin", "gqB.f",
)


def nn(a, b):
    return jnp.dot(a, b, preferred_element_type=F32)


def nt(a, b):
    return lax.dot_general(a, b, (((1,), (1,)), ((), ())), preferred_element_type=F32)


def tn(a, b):
    return lax.dot_general(a, b, (((0,), (0,)), ((), ())), preferred_element_type=F32)


def kernel(
    anchor, augment, lag_in, w_query, w_key, w_value, w_out, cot_in,
    update_hbm, g_query_hbm, g_key_hbm, g_value_hbm, g_out_hbm,
    anc, anc_t, sts, sts_t, cot, wq, wkv, wo,
    s_out, s_kv, s_q, upd, rz, ru,
    ra_out, rc_out, ry_out, ra_kv, rc_kv, ry_kv, ra_q, rc_q, ry_q,
    part, part_kv, other, other_kv, q_h, k_h, v_h, b_h, probs, att, ctx, qb, kvb,
    update, g_query, g_key, g_value, g_out, lag,
    send, recv, near_send, near_recv, fin_recv, local,
):
    dp, c, t = lax.axis_index("dp"), lax.axis_index("seq"), lax.axis_index("tensor")
    z, yl = t // 2, t % 2
    o = 1 - c
    xr, xl = (dp + 2) % NS, (dp + 6) % NS
    far = (dp + 4) % NS
    yp = dp + 1 - 2 * (dp % 2)
    ty = t + 1 - 2 * yl
    to_xr, to_xl, to_yp = (xr, c, t), (xl, c, t), (yp, c, t)
    to_zr, to_zl = (dp, c, (t + 2) % 16), (dp, c, (t + 14) % 16)
    to_sib = (dp, o, t)
    same = c == yl

    barrier = pltpu.get_barrier_semaphore()
    partners = (to_xr, to_xl, to_yp, to_zr, to_zl, to_sib, (dp, 0, ty), (dp, 1, ty))
    for who in partners:
        pl.semaphore_signal(barrier, inc=1, device_id=who, device_id_type=MESH)
    pl.semaphore_wait(barrier, len(partners))

    started = []
    arriving = {}
    tasks = {}

    def push(name, src, dst, who):
        i = len(started)
        copy = pltpu.make_async_remote_copy(
            src_ref=src, dst_ref=dst, send_sem=send.at[i], recv_sem=recv.at[i],
            device_id=who, device_id_type=MESH,
        )
        copy.start()
        started.append(copy)
        arriving.setdefault(name, []).append(copy)

    def wait(*names):
        for name in names:
            for copy in arriving.pop(name, ()):
                copy.wait_recv()

    locals_ = []

    def fetch(src, dst):
        copy = pltpu.make_async_copy(src, dst, local.at[len(locals_)])
        copy.start()
        locals_.append(copy)

    def col(i, n):
        return pl.ds(pl.multiple_of(i * n, n), n)

    def flip(k):
        return k + 1 - 2 * (k % 2)

    mine = pl.ds(pl.multiple_of(c * TOK, TOK), TOK)
    head = col(c, HEAD)
    head_o = col(o, HEAD)
    head_v = pl.ds(pl.multiple_of(256 + c * HEAD, HEAD), HEAD)
    head_vo = pl.ds(pl.multiple_of(256 + o * HEAD, HEAD), HEAD)

    def kv_rows(k, r0, n):
        return pl.ds(pl.multiple_of((2 * k + c) * 224 + r0, 16), n)

    def rows_of(buf):
        return lambda k, r0, n: buf.at[k, pl.ds(r0, n)]

    def slot_kv(k, r0, n):
        return wkv.at[kv_rows(k, r0, n)]

    def y_first(name, own, slot, r0, n):
        h = n // 2

        def from_y():
            wait(name + "y")
            s = slot(yp, r0, n)
            push(name + "fr", s, s, to_xr)
            push(name + "fl", s, s, to_xl)

        def near(first, second, a, b):
            def run():
                wait(name + first + "r", name + first + "l")
                lo, hi = slot(a, r0, h), slot(b, r0 + h, h)
                push(name + second + "0", lo, lo, to_xr)
                push(name + second + "1", hi, hi, to_xl)
            return run

        tasks[name + ".fy"] = from_y
        tasks[name + ".fx"] = near("", "h", xl, xr)
        tasks[name + ".fxf"] = near("f", "g", flip(xl), flip(xr))
        for src, dst in own:
            push(name + "y", src, dst, to_yp)
        for src, dst in own:
            push(name + "r", src, dst, to_xr)
            push(name + "l", src, dst, to_xl)
        return [name + e for e in ("y", "r", "l", "fr", "fl", "h0", "h1", "g0", "g1")]

    def x_first(name, own, slot, r0, n):
        h = n // 2

        def from_x():
            wait(name + "r", name + "l")
            lo, hi = slot(xl, r0, h), slot(xr, r0 + h, h)
            push(name + "h0", lo, lo, to_xr)
            push(name + "h1", hi, hi, to_xl)
            a, b = slot(xl, r0, n), slot(xr, r0, n)
            push(name + "y0", a, a, to_yp)
            push(name + "y1", b, b, to_yp)

        def from_far():
            for i in (0, 1):
                wait(name + "h%d" % i)
                s = slot(far, r0 + i * h, h)
                push(name + "g%d" % i, s, s, to_yp)

        tasks[name + ".fx"] = from_x
        tasks[name + ".fxf"] = from_far
        for src, dst in own:
            push(name + "r", src, dst, to_xr)
            push(name + "l", src, dst, to_xl)
        for src, dst in own:
            push(name + "y", src, dst, to_yp)
        return [name + e for e in ("y", "r", "l", "h0", "h1", "y0", "y1", "g0", "g1")]

    def own_rows(src, buf, r0, n):
        return [(src.at[pl.ds(r0, n)], buf.at[dp, pl.ds(r0, n)])]

    def split(name, src, buf, cut):
        n = buf.shape[1]
        names = []
        if cut:
            names += x_first(name + "A", own_rows(src, buf, 0, cut), rows_of(buf), 0, cut)
        if cut < n:
            names += y_first(name + "B", own_rows(src, buf, cut, n - cut), rows_of(buf), cut, n - cut)
        return names

    cot_dst = cot.at[z, mine]
    cot_far = pltpu.make_async_remote_copy(
        src_ref=cot_in.at[0], dst_ref=cot_dst, send_sem=near_send.at[0], recv_sem=near_recv.at[c],
        device_id=(dp, yl, ty), device_id_type=MESH)
    cot_sib = pltpu.make_async_remote_copy(
        src_ref=cot_in.at[0], dst_ref=cot_dst, send_sem=near_send.at[1], recv_sem=near_recv.at[c],
        device_id=to_sib, device_id_type=MESH)
    cot_own = pltpu.make_async_copy(cot_in.at[0], cot_dst, near_recv.at[c])
    cot_far.start()

    @pl.when(same)
    def _():
        cot_own.start()

    @pl.when(jnp.logical_not(same))
    def _():
        cot_sib.start()

    own_kv = kv_rows(dp, 0, 224)
    kv_all = y_first("kv", [(w_key, wkv.at[own_kv, pl.ds(0, 256)]), (w_value, wkv.at[own_kv, pl.ds(256, 256)])],
                     slot_kv, 0, 224)
    q_all = split("q", w_query, wq, Q_Y)
    o_all = []

    def own_o():
        o_all.extend(split("o", w_out, wo, O_Y))

    tasks["own_o"] = own_o

    push("sib", augment.at[0], sts.at[mine], to_sib)
    fetch(augment.at[0], sts.at[mine])
    for k in range(NS):
        push("sib", anchor.at[0, :, pl.ds(pl.multiple_of((2 * k + o) * 512, 512), 512)], anc.at[k, mine], to_sib)
        fetch(anchor.at[0, :, pl.ds(pl.multiple_of((2 * k + c) * 512, 512), 512)], anc.at[k, mine])
    fetch(w_query, wq.at[dp])
    fetch(w_key, wkv.at[own_kv, pl.ds(0, 256)])
    fetch(w_value, wkv.at[own_kv, pl.ds(256, 256)])
    fetch(w_out, wo.at[dp])
    fetch(lag_in, lag)

    zero = jnp.zeros((224, 512), BF)
    for k in range(NS):
        wkv[pl.ds(pl.multiple_of((2 * k + o) * 224, 224), 224), :] = zero

    lo_tok, hi_tok = pl.ds(0, TOK), pl.ds(TOK, TOK)

    def ring(step, part_):
        def run():
            a, b = (lo_tok, hi_tok) if part_ == "a" else (hi_tok, lo_tok)
            if step == 1 and part_ == "a":
                for h in (0, 1):
                    got = cot.at[z, pl.ds(h * TOK, TOK)]
                    pltpu.make_async_copy(got, got, near_recv.at[h]).wait()
            if step > 1:
                wait("Z%d%s" % (step - 1, part_))
            s, r = cot.at[(z + 9 - step) % NS, a], cot.at[(z + step - 1) % NS, b]
            push("Z%d%s" % (step, part_), s, s, to_zr)
            push("Z%d%s" % (step, part_), r, r, to_zl)
        return run

    z_all = []
    for step in range(1, 5):
        for part_ in ("a", "b") if step < 4 else ("a",):
            tasks["z%d%s" % (step, part_)] = ring(step, part_)
            z_all.append("Z%d%s" % (step, part_))

    def turn(i):
        def run():
            if i == 0:
                wait("sib")
                for copy in locals_:
                    copy.wait()
            anc_t[i] = anc[i].T
            if i < 7:
                sts_t[pl.ds(i * 512, 512), :] = sts[:, pl.ds(i * 512, 512)].T
        return run

    for i in range(NS):
        tasks["turn%d" % i] = turn(i)

    def keys_values():
        wait(*kv_all)
        part_kv[...] = nn(sts[:, pl.ds(0, 512)], wkv[pl.ds(0, 512), :])

        def add_kv(j, _):
            part_kv[...] += nn(sts[:, col(j, 512)], wkv[col(j, 512), :])
            return _

        lax.fori_loop(1, 7, add_kv, 0)
        push("exk", part_kv.at[:, head_o], other_kv.at[0], to_sib)
        push("exk", part_kv.at[:, head_vo], other_kv.at[1], to_sib)

    def queries():
        wait(*q_all)
        part[0] = nn(anc[0], wq[0])

        def add_q(k, _):
            part[0] += nn(anc[k], wq[k])
            return _

        lax.fori_loop(1, NS, add_q, 0)
        push("exq", part.at[0, :, head_o], other.at[0], to_sib)

    factor = HEAD ** (-0.5)
    block = 128

    def attend(r):
        def run():
            if r == 0:
                wait("exk")
                k_h[...] = (part_kv[:, head] + other_kv[0]).astype(BF)
                v_h[...] = (part_kv[:, head_v] + other_kv[1]).astype(BF)
                wait("exq")
                q_h[...] = (part[0, :, head] + other[0]).astype(BF)
            rows = pl.ds(r * block, block)
            scores = nt(q_h[rows, :], k_h[...]) * factor
            reach = lax.broadcasted_iota(jnp.int32, (block, LEN), 0) + (r * block + lag[0])
            allowed = lax.broadcasted_iota(jnp.int32, (block, LEN), 1) <= reach
            scores = jnp.where(allowed, scores, -jnp.inf)
            expo = jnp.exp(scores - jnp.max(scores, axis=1, keepdims=True))
            p = expo / jnp.sum(expo, axis=1, keepdims=True)
            probs[rows, :] = p
            a = p.astype(BF)
            att[rows, :] = a
            ctx[rows, head] = nn(a, v_h[...]).astype(BF)
            if r == LEN // block - 1:
                push("ectx", ctx.at[:, head], ctx.at[:, head], to_sib)
        return run

    tasks["kv"] = keys_values
    tasks["q"] = queries
    for r in range(LEN // block):
        tasks["attn%d" % r] = attend(r)

    def back_context():
        wait(*o_all)
        wait(*z_all)
        part[1] = nt(cot[0], wo[0])

        def add_b(k, _):
            part[1] += nt(cot[k], wo[k])
            return _

        lax.fori_loop(1, NS, add_b, 0)
        push("eb", part.at[1, :, head_o], other.at[1], to_sib)

    tasks["bc"] = back_context

    def backward(r):
        def run():
            if r == 0:
                wait("eb")
                b_h[...] = (part[1, :, head] + other[1]).astype(BF)
            rows = pl.ds(r * block, block)
            dprobs = nt(b_h[rows, :], v_h[...])
            delta = jnp.sum(b_h[rows, :].astype(F32) * ctx[rows, head].astype(F32), axis=1, keepdims=True)
            ds = (probs[rows, :] * (dprobs - delta) * factor).astype(BF)
            qb[rows, head] = nn(ds, k_h[...]).astype(BF)
            kt = tn(ds, q_h[rows, :])
            vt = tn(att[rows, :], b_h[rows, :])
            if r == 0:
                other_kv[0] = kt
                other_kv[1] = vt
            else:
                other_kv[0] += kt
                other_kv[1] += vt
            if r == LEN // block - 1:
                kvb[:, head] = other_kv[0].astype(BF)
                kvb[:, head_v] = other_kv[1].astype(BF)
                push("ekb", kvb.at[:, head], kvb.at[:, head], to_sib)
                push("ekb", kvb.at[:, head_v], kvb.at[:, head_v], to_sib)
                push("ekb", qb.at[:, head], qb.at[:, head], to_sib)
        return run

    for r in range(LEN // block):
        tasks["bwd%d" % r] = backward(r)

    def slot(off, j):
        k = (dp + 2 * off + NS) % NS
        return flip(k) if j else k

    def add(s, k, rows, got):
        s[k, rows] = (s[k, rows].astype(F32) + got.astype(F32)).astype(BF)

    def sum_x_first(name, ready, s, r0, n, ra, rc, ry, make, out):
        h = n // 2
        lo, hi = pl.ds(r0, h), pl.ds(r0 + h, h)
        full = pl.ds(r0, n)

        def first(j):
            def run():
                ready()
                k = slot(2, j)
                make(k, r0, n)
                push(name + "a%d" % j, s.at[k, lo], ra.at[0, j], to_xr)
                push(name + "a%d" % j, s.at[k, hi], ra.at[1, j], to_xl)
            return run

        def second(j):
            def run():
                k, m = slot(1, j), slot(-1, j)
                make(k, r0, n)
                push(name + "b%d" % j, s.at[k, hi], rc.at[0, j, pl.ds(h, h)], to_xr)
                make(m, r0, n)
                push(name + "b%d" % j, s.at[m, lo], rc.at[1, j, pl.ds(0, h)], to_xl)
            return run

        def own():
            make(slot(0, 1), r0, n)
            make(slot(0, 0), r0, n)

        def on(j):
            def run():
                wait(name + "a%d" % j)
                k, m = slot(1, j), slot(-1, j)
                add(s, k, lo, ra[0, j])
                push(name + "p%d" % j, s.at[k, lo], rc.at[0, j, pl.ds(0, h)], to_xr)
                add(s, m, hi, ra[1, j])
                push(name + "p%d" % j, s.at[m, hi], rc.at[1, j, pl.ds(h, h)], to_xl)
            return run

        def total(j):
            wait(name + "b%d" % j, name + "p%d" % j)
            return s[slot(0, j), full].astype(F32) + rc[0, j].astype(F32) + rc[1, j].astype(F32)

        def across():
            k = slot(0, 1)
            s[k, full] = total(1).astype(BF)
            push(name + "y", s.at[k, full], ry, to_yp)

        def finish():
            both = total(0)
            wait(name + "y")
            out(both + ry[...].astype(F32), r0, n)

        for j in (0, 1):
            tasks[name + ".a%d" % j] = first(j)
            tasks[name + ".b%d" % j] = second(j)
            tasks[name + ".p%d" % j] = on(j)
        tasks[name + ".m0"] = own
        tasks[name + ".y"] = across
        tasks[name + ".f"] = finish

    def sum_y_first(name, ready, s, r0, n, ra, rc, ry, make, out):
        h = n // 2
        lo, hi = pl.ds(r0, h), pl.ds(r0 + h, h)
        full = pl.ds(r0, n)
        offs = (2, 1, -1, 0)

        def first(i):
            def run():
                ready()
                k = slot(offs[i], 1)
                make(k, r0, n)
                push(name + "y%d" % i, s.at[k, full], ry.at[i], to_yp)
            return run

        def own():
            for off in offs:
                make(slot(off, 0), r0, n)

        def from_y():
            wait(name + "y0")
            k = slot(2, 0)
            add(s, k, full, ry[0])
            push(name + "a", s.at[k, lo], ra.at[0], to_xr)
            push(name + "a_", s.at[k, hi], ra.at[1], to_xl)

        def right():
            wait(name + "y1")
            k = slot(1, 0)
            add(s, k, full, ry[1])
            push(name + "b", s.at[k, hi], rc.at[0, pl.ds(h, h)], to_xr)

        def left():
            wait(name + "y2")
            m = slot(-1, 0)
            add(s, m, full, ry[2])
            push(name + "b", s.at[m, lo], rc.at[1, pl.ds(0, h)], to_xl)

        def on_right():
            wait(name + "a")
            k = slot(1, 0)
            add(s, k, lo, ra[0])
            push(name + "p", s.at[k, lo], rc.at[0, pl.ds(0, h)], to_xr)

        def on_left():
            wait(name + "a_")
            m = slot(-1, 0)
            add(s, m, hi, ra[1])
            push(name + "p", s.at[m, hi], rc.at[1, pl.ds(h, h)], to_xl)

        def finish():
            wait(name + "y3", name + "b", name + "p")
            k = slot(0, 0)
            out(s[k, full].astype(F32) + ry[3].astype(F32) + rc[0].astype(F32) + rc[1].astype(F32), r0, n)

        for i in range(4):
            tasks[name + ".y%d" % i] = first(i)
        tasks[name + ".m"] = own
        tasks[name + ".a"] = from_y
        tasks[name + ".b"] = right
        tasks[name + ".b_"] = left
        tasks[name + ".p"] = on_right
        tasks[name + ".p_"] = on_left
        tasks[name + ".f"] = finish

    written = []

    def write(src, dst):
        copy = pltpu.make_async_copy(src, dst, fin_recv.at[2 + len(written)])
        copy.start()
        written.append(copy)

    def make_out(k, r0, n):
        s_out[k, pl.ds(r0, n)] = tn(ctx[:, pl.ds(r0, n)], cot[k]).astype(BF)

    def put_out(total, r0, n):
        g_out[pl.ds(r0, n)] = total.astype(BF)
        write(g_out.at[pl.ds(r0, n)], g_out_hbm.at[pl.ds(r0, n)])

    def make_kv(k, r0, n):
        s_kv[k] = nn(sts_t[pl.ds(pl.multiple_of((2 * k + c) * 224, 224), 224), :], kvb[...]).astype(BF)

    def put_kv(total, r0, n):
        g_key[...] = total[:, :256].astype(BF)
        g_value[...] = total[:, 256:].astype(BF)
        write(g_key, g_key_hbm)
        write(g_value, g_value_hbm)

    def make_q(k, r0, n):
        s_q[k, pl.ds(r0, n)] = nn(anc_t[k, pl.ds(r0, n), :], qb[...]).astype(BF)

    def put_q(total, r0, n):
        g_query[pl.ds(r0, n)] = total.astype(BF)
        write(g_query.at[pl.ds(r0, n)], g_query_hbm.at[pl.ds(r0, n)])

    def ctx_ready():
        wait(*z_all)
        wait("ectx")

    def back_ready():
        wait("ekb")

    ra_oa, ra_ob = ra_out
    rc_oa, rc_ob = rc_out
    ry_oa, ry_ob = ry_out
    ra_qa, ra_qb = ra_q
    rc_qa, rc_qb = rc_q
    ry_qa, ry_qb = ry_q
    if GO_Y:
        sum_y_first("goA", ctx_ready, s_out, 0, GO_Y, ra_oa, rc_oa, ry_oa, make_out, put_out)
    if GO_Y < 256:
        sum_x_first("goB", ctx_ready, s_out, GO_Y, 256 - GO_Y, ra_ob, rc_ob, ry_ob, make_out, put_out)
    sum_x_first("gkv", back_ready, s_kv, 0, 224, ra_kv, rc_kv, ry_kv, make_kv, put_kv)
    if GQ_Y:
        sum_y_first("gqA", back_ready, s_q, 0, GQ_Y, ra_qa, rc_qa, ry_qa, make_q, put_q)
    if GQ_Y < 512:
        sum_x_first("gqB", back_ready, s_q, GQ_Y, 512 - GQ_Y, ra_qb, rc_qb, ry_qb, make_q, put_q)

    def ring_add(step, part_):
        def run():
            a, b = (lo_tok, hi_tok) if part_ == "a" else (hi_tok, lo_tok)
            k, m = (z + 5 - step) % NS, (z + 3 + step) % NS
            if step > 1 and (step, part_) != (2, "b"):
                wait("U%d%s" % (step - 1, part_))
                add(upd, k, a, rz[0, step - 2, a])
                push("U%d%s" % (step, part_), upd.at[k, a], rz.at[0, step - 1, a], to_zr)
                add(upd, m, b, rz[1, step - 2, b])
                push("U%d%s" % (step, part_), upd.at[m, b], rz.at[1, step - 1, b], to_zl)
            else:
                push("U%d%s" % (step, part_), upd.at[k, a], rz.at[0, step - 1, a], to_zr)
                push("U%d%s" % (step, part_), upd.at[m, b], rz.at[1, step - 1, b], to_zl)
        return run

    def updates():
        wait("ectx")
        wait(*o_all)

        def make_upd(k, _):
            upd[k] = nn(ctx[...], wo[k]).astype(BF)
            return _

        lax.fori_loop(0, NS, make_upd, 0)
        ring_add(1, "a")()
        ring_add(2, "b")()

    tasks["upd"] = updates
    for step in (2, 3, 4):
        for part_ in ("a", "b"):
            if (step, part_) != (2, "b"):
                tasks["u%d%s" % (step, part_)] = ring_add(step, part_)

    given = upd.at[z, pl.ds(pl.multiple_of(o * TOK, TOK), TOK)]
    fin_own = pltpu.make_async_copy(upd.at[z, mine], ru.at[0], fin_recv.at[0])
    fin_sib = pltpu.make_async_remote_copy(
        src_ref=given, dst_ref=ru.at[0], send_sem=near_send.at[2], recv_sem=fin_recv.at[0],
        device_id=to_sib, device_id_type=MESH)
    fin_far = [
        pltpu.make_async_remote_copy(
            src_ref=upd.at[z, pl.ds(h * TOK, TOK)], dst_ref=ru.at[1], send_sem=near_send.at[3 + h],
            recv_sem=fin_recv.at[1], device_id=(dp, h, ty), device_id_type=MESH)
        for h in (0, 1)
    ]

    def last_exchange():
        wait("U4a", "U4b")
        upd[z] = (upd[z].astype(F32) + rz[0, 3].astype(F32) + rz[1, 3].astype(F32)).astype(BF)

        @pl.when(same)
        def _():
            fin_own.start()
            fin_sib.start()

        @pl.when(jnp.logical_not(same))
        def _():
            fin_far[0].start()
            fin_far[1].start()

    def last_sum():
        for i in (0, 1):
            pltpu.make_async_copy(ru.at[i], ru.at[i], fin_recv.at[i]).wait()
        update[0] = (ru[0].astype(F32) + ru[1].astype(F32)).astype(BF)
        write(update, update_hbm)

    tasks["u5"] = last_exchange
    tasks["ufin"] = last_sum

    for name in ORDER:
        tasks.pop(name)()
    assert not tasks and not arriving

    for copy in started:
        copy.wait_send()
    cot_far.wait_send()

    @pl.when(jnp.logical_not(same))
    def _():
        cot_sib.wait_send()
        fin_far[0].wait_send()
        fin_far[1].wait_send()

    @pl.when(same)
    def _():
        fin_sib.wait_send()

    for copy in written:
        copy.wait()


def hand_on(*refs):
    for i in range(5):
        refs[5 + i][...] = refs[i][...]


def local(*args):
    vm = pltpu.VMEM
    shapes = [
        ((1, TOK, 512), BF), ((512, 256), BF), ((224, 256), BF), ((224, 256), BF), ((256, 512), BF),
    ]

    def landing(n, width, cut):
        a, b = max(cut, 32), max(n - cut, 32)
        ra = [vm((2, a // 2, width), BF), vm((2, 2, b // 2, width), BF)]
        rc = [vm((2, a, width), BF), vm((2, 2, b, width), BF)]
        ry = [vm((4, a, width), BF), vm((b, width), BF)]
        return [ra, rc, ry]

    scratch = [
        vm((NS, LEN, 512), BF), vm((NS, 512, LEN), BF), vm((LEN, 3584), BF), vm((3584, LEN), BF),
        vm((NS, LEN, 512), BF), vm((NS, 512, 256), BF), vm((3584, 512), BF), vm((NS, 256, 512), BF),
        vm((NS, 256, 512), BF), vm((NS, 224, 512), BF), vm((NS, 512, 256), BF),
        vm((NS, LEN, 512), BF), vm((2, 4, LEN, 512), BF), vm((2, TOK, 512), BF),
        *landing(256, 512, GO_Y),
        vm((2, 2, 112, 512), BF), vm((2, 2, 224, 512), BF), vm((224, 512), BF),
        *landing(512, 256, GQ_Y),
        vm((2, LEN, 256), F32), vm((LEN, 512), F32), vm((2, LEN, HEAD), F32), vm((2, LEN, HEAD), F32),
        vm((LEN, HEAD), BF), vm((LEN, HEAD), BF), vm((LEN, HEAD), BF), vm((LEN, HEAD), BF),
        vm((LEN, LEN), F32), vm((LEN, LEN), BF), vm((LEN, 256), BF), vm((LEN, 256), BF), vm((LEN, 512), BF),
        vm((1, TOK, 512), BF), vm((512, 256), BF), vm((224, 256), BF), vm((224, 256), BF), vm((256, 512), BF),
        pltpu.SMEM((1,), jnp.int32),
        pltpu.SemaphoreType.DMA((COPIES,)), pltpu.SemaphoreType.DMA((COPIES,)),
        pltpu.SemaphoreType.DMA((5,)), pltpu.SemaphoreType.DMA((2,)), pltpu.SemaphoreType.DMA((9,)),
        pltpu.SemaphoreType.DMA((16,)),
    ]
    any_ = pl.BlockSpec(memory_space=pl.ANY)
    vmem = pl.BlockSpec(memory_space=pltpu.VMEM)
    results = [jax.ShapeDtypeStruct(s, d) for s, d in shapes]
    outs = pl.pallas_call(
        kernel,
        out_shape=results,
        in_specs=[any_] * 8,
        out_specs=[any_] * 5,
        scratch_shapes=scratch,
        compiler_params=pltpu.CompilerParams(
            collective_id=0, has_side_effects=True, vmem_limit_bytes=58 * 2**20
        ),
        name="block",
    )(*args)
    return pl.pallas_call(
        hand_on,
        out_shape=results,
        in_specs=[vmem] * 5,
        out_specs=[vmem] * 5,
        name="hand_on",
    )(*outs)


def solution(mesh):
    placed = (
        P("dp", "seq", None),
        P("dp", "seq", None),
        P("dp"),
        P(("dp", "seq"), "tensor"),
        P(("dp", "seq"), "tensor"),
        P(("dp", "seq"), "tensor"),
        P("tensor", ("dp", "seq")),
        P("dp", "seq", "tensor"),
    )
    return jax.shard_map(
        local,
        mesh=mesh,
        in_specs=placed,
        out_specs=(
            P("dp", "seq", "tensor"),
            P(("dp", "seq"), "tensor"),
            P(("dp", "seq"), "tensor"),
            P(("dp", "seq"), "tensor"),
            P("tensor", ("dp", "seq")),
        ),
        check_vma=False,
    )
```

```python
import jax
import jax.numpy as jnp
from jax import lax
from jax.experimental import pallas as pl
from jax.experimental.pallas import tpu as pltpu
from jax.sharding import PartitionSpec as P

MESH = pl.DeviceIdType.MESH
BF = jnp.bfloat16
F32 = jnp.float32
HEAD = 128
TOK = 192
LEN = 384
NS = 8
COPIES = 256

Q_Y, O_Y, GQ_Y, GO_Y = 416, 96, 416, 128

FIRST = ('kv', 'qA', 'qB')
O_LAST_Y = 1

ORDER = (
    "z1a", "z1b", "kv.fx", "kv.fy", "qA.fx", "qB.fx", "z2a", "turn0", "turn1", "turn2", "turn3", "turn4",
    "turn5", "qB.fy", "turn6", "z2b", "turn7", "kv.fxf", "z3a", "qA.fxf", "own_o", "qB.fxf", "z3b", "kv",
    "z4a", "oB.fx", "oA.fx", "q", "oB.fy", "oA.fxf", "attn0", "attn1", "attn2", "oB.fxf", "goA.y0", "goA.y1",
    "goA.y2", "goA.y3", "goB.a0", "goB.a1", "goB.b0", "goB.b1", "goA.m", "goB.m0", "bc", "upd", "goA.a",
    "goB.p0", "goB.p1", "bwd0", "bwd1", "bwd2", "goA.b", "goA.b_", "goA.p", "goA.p_", "u2a", "goB.y",
    "gkv.a0", "gkv.a1", "gqA.y0", "gqA.y1", "gqA.y2", "gqA.y3", "gkv.b0", "gkv.b1", "u3b", "gqB.a0", "gqB.a1",
    "gqB.b0", "gqB.b1", "gkv.m0", "gqA.m", "goA.f", "goB.f", "gqB.m0", "gkv.p0", "u3a", "gkv.p1", "gqA.a",
    "u4b", "gqB.p0", "gqA.b", "gqB.p1", "u4a", "gqA.b_", "gkv.y", "gqA.p", "gqA.p_", "u5", "gqB.y", "gkv.f",
    "gqA.f", "ufin", "gqB.f",
)


def nn(a, b):
    return jnp.dot(a, b, preferred_element_type=F32)


def nt(a, b):
    return lax.dot_general(a, b, (((1,), (1,)), ((), ())), preferred_element_type=F32)


def tn(a, b):
    return lax.dot_general(a, b, (((0,), (0,)), ((), ())), preferred_element_type=F32)


def kernel(
    anchor, augment, lag_in, w_query, w_key, w_value, w_out, cot_in,
    update, g_query, g_key, g_value, g_out,
    anc, anc_t, sts, sts_t, cot, wq, wkv, wo,
    s_out, s_kv, s_q, upd, rz, ru,
    ra_out, rc_out, ry_out, ra_kv, rc_kv, ry_kv, ra_q, rc_q, ry_q,
    part, part_kv, other, other_kv, q_h, k_h, v_h, b_h, probs, att, ctx, qb, kvb,
    lag, stage,
    send, recv, near_send, near_recv, fin_recv, local,
):
    dp, c, t = lax.axis_index("dp"), lax.axis_index("seq"), lax.axis_index("tensor")
    z, yl = t // 2, t % 2
    o = 1 - c
    xr, xl = (dp + 2) % NS, (dp + 6) % NS
    far = (dp + 4) % NS
    yp = dp + 1 - 2 * (dp % 2)
    ty = t + 1 - 2 * yl
    to_xr, to_xl, to_yp = (xr, c, t), (xl, c, t), (yp, c, t)
    to_zr, to_zl = (dp, c, (t + 2) % 16), (dp, c, (t + 14) % 16)
    to_sib = (dp, o, t)
    same = c == yl

    barrier = pltpu.get_barrier_semaphore()
    partners = (to_xr, to_xl, to_yp, to_zr, to_zl, to_sib, (dp, 0, ty), (dp, 1, ty))
    for who in partners:
        pl.semaphore_signal(barrier, inc=1, device_id=who, device_id_type=MESH)

    started = []
    arriving = {}
    tasks = {}

    def push(name, src, dst, who):
        i = len(started)
        copy = pltpu.make_async_remote_copy(
            src_ref=src, dst_ref=dst, send_sem=send.at[i], recv_sem=recv.at[i],
            device_id=who, device_id_type=MESH,
        )
        copy.start()
        started.append(copy)
        arriving.setdefault(name, []).append(copy)

    def wait(*names):
        for name in names:
            for copy in arriving.pop(name, ()):
                copy.wait_recv()

    locals_ = []

    def fetch(src, dst):
        copy = pltpu.make_async_copy(src, dst, local.at[len(locals_)])
        copy.start()
        locals_.append(copy)

    def col(i, n):
        return pl.ds(pl.multiple_of(i * n, n), n)

    def flip(k):
        return k + 1 - 2 * (k % 2)

    mine = pl.ds(pl.multiple_of(c * TOK, TOK), TOK)
    head = col(c, HEAD)
    head_o = col(o, HEAD)
    head_v = pl.ds(pl.multiple_of(256 + c * HEAD, HEAD), HEAD)
    head_vo = pl.ds(pl.multiple_of(256 + o * HEAD, HEAD), HEAD)

    def kv_rows(k, r0, n):
        return pl.ds(pl.multiple_of((2 * k + c) * 224 + r0, 16), n)

    def rows_of(buf):
        return lambda k, r0, n: buf.at[k, pl.ds(r0, n)]

    def slot_kv(k, r0, n):
        return wkv.at[kv_rows(k, r0, n)]

    def y_first(name, slot, r0, n):
        h = n // 2
        mine_ = slot(dp, r0, n)

        def from_y():
            wait(name + "y")
            s = slot(yp, r0, n)
            push(name + "fr", s, s, to_xr)
            push(name + "fl", s, s, to_xl)

        def near(first, second, a, b):
            def run():
                wait(name + first + "r", name + first + "l")
                lo, hi = slot(a, r0, h), slot(b, r0 + h, h)
                push(name + second + "0", lo, lo, to_xr)
                push(name + second + "1", hi, hi, to_xl)
            return run

        tasks[name + ".fy"] = from_y
        tasks[name + ".fx"] = near("", "h", xl, xr)
        tasks[name + ".fxf"] = near("f", "g", flip(xl), flip(xr))
        push(name + "y", mine_, mine_, to_yp)
        push(name + "r", mine_, mine_, to_xr)
        push(name + "l", mine_, mine_, to_xl)
        return [name + e for e in ("y", "r", "l", "fr", "fl", "h0", "h1", "g0", "g1")]

    def x_first(name, slot, r0, n):
        h = n // 2
        mine_ = slot(dp, r0, n)

        def from_x():
            wait(name + "r", name + "l")
            lo, hi = slot(xl, r0, h), slot(xr, r0 + h, h)
            push(name + "h0", lo, lo, to_xr)
            push(name + "h1", hi, hi, to_xl)
            a, b = slot(xl, r0, n), slot(xr, r0, n)
            push(name + "y0", a, a, to_yp)
            push(name + "y1", b, b, to_yp)

        def from_far():
            for i in (0, 1):
                wait(name + "h%d" % i)
                s = slot(far, r0 + i * h, h)
                push(name + "g%d" % i, s, s, to_yp)

        tasks[name + ".fx"] = from_x
        tasks[name + ".fxf"] = from_far
        push(name + "r", mine_, mine_, to_xr)
        push(name + "l", mine_, mine_, to_xl)
        push(name + "y", mine_, mine_, to_yp)
        return [name + e for e in ("y", "r", "l", "h0", "h1", "y0", "y1", "g0", "g1")]

    own_kv = kv_rows(dp, 0, 224)
    fetch(cot_in.at[0], stage)
    fetch(w_key, wkv.at[own_kv, pl.ds(0, 256)])
    fetch(w_value, wkv.at[own_kv, pl.ds(256, 256)])
    fetch(w_query, wq.at[dp])
    fetch(w_out, wo.at[dp])
    early = len(locals_)
    fetch(lag_in, lag)
    for copy in locals_[:early]:
        copy.wait()
    pl.semaphore_wait(barrier, len(partners))

    cot_dst = cot.at[z, mine]
    cot_far = pltpu.make_async_remote_copy(
        src_ref=stage, dst_ref=cot_dst, send_sem=near_send.at[0], recv_sem=near_recv.at[c],
        device_id=(dp, yl, ty), device_id_type=MESH)
    cot_sib = pltpu.make_async_remote_copy(
        src_ref=stage, dst_ref=cot_dst, send_sem=near_send.at[1], recv_sem=near_recv.at[c],
        device_id=to_sib, device_id_type=MESH)
    cot_own = pltpu.make_async_copy(stage, cot_dst, near_recv.at[c])
    cot_far.start()

    @pl.when(same)
    def _():
        cot_own.start()

    @pl.when(jnp.logical_not(same))
    def _():
        cot_sib.start()

    kv_all, q_all, o_all = [], [], []

    def gather_q_a():
        if Q_Y:
            q_all.extend(x_first("qA", rows_of(wq), 0, Q_Y))

    def gather_q_b():
        if Q_Y < 512:
            q_all.extend(y_first("qB", rows_of(wq), Q_Y, 512 - Q_Y))

    def gather_kv():
        kv_all.extend(y_first("kv", slot_kv, 0, 224))

    first = {"kv": gather_kv, "qA": gather_q_a, "qB": gather_q_b}
    for name in FIRST:
        first[name]()

    def gather_o_a():
        if O_Y:
            o_all.extend(x_first("oA", rows_of(wo), 0, O_Y))

    def gather_o_b():
        if O_Y < 256:
            o_all.extend(y_first("oB", rows_of(wo), O_Y, 256 - O_Y))

    def own_o():
        for run in (gather_o_b, gather_o_a) if O_LAST_Y else (gather_o_a, gather_o_b):
            run()

    tasks["own_o"] = own_o

    push("sib", augment.at[0], sts.at[mine], to_sib)
    fetch(augment.at[0], sts.at[mine])
    for k in range(NS):
        push("sib", anchor.at[0, :, pl.ds(pl.multiple_of((2 * k + o) * 512, 512), 512)], anc.at[k, mine], to_sib)
        fetch(anchor.at[0, :, pl.ds(pl.multiple_of((2 * k + c) * 512, 512), 512)], anc.at[k, mine])

    zero = jnp.zeros((224, 512), BF)
    for k in range(NS):
        wkv[pl.ds(pl.multiple_of((2 * k + o) * 224, 224), 224), :] = zero

    lo_tok, hi_tok = pl.ds(0, TOK), pl.ds(TOK, TOK)

    def ring(step, part_):
        def run():
            a, b = (lo_tok, hi_tok) if part_ == "a" else (hi_tok, lo_tok)
            if step == 1 and part_ == "a":
                for h in (0, 1):
                    got = cot.at[z, pl.ds(h * TOK, TOK)]
                    pltpu.make_async_copy(got, got, near_recv.at[h]).wait()
            if step > 1:
                wait("Z%d%s" % (step - 1, part_))
            s, r = cot.at[(z + 9 - step) % NS, a], cot.at[(z + step - 1) % NS, b]
            push("Z%d%s" % (step, part_), s, s, to_zr)
            push("Z%d%s" % (step, part_), r, r, to_zl)
        return run

    z_all = []
    for step in range(1, 5):
        for part_ in ("a", "b") if step < 4 else ("a",):
            tasks["z%d%s" % (step, part_)] = ring(step, part_)
            z_all.append("Z%d%s" % (step, part_))

    def turn(i):
        def run():
            if i == 0:
                wait("sib")
                for copy in locals_[early:]:
                    copy.wait()
            anc_t[i] = anc[i].T
            if i < 7:
                sts_t[pl.ds(i * 512, 512), :] = sts[:, pl.ds(i * 512, 512)].T
        return run

    for i in range(NS):
        tasks["turn%d" % i] = turn(i)

    def keys_values():
        wait(*kv_all)
        part_kv[...] = nn(sts[:, pl.ds(0, 512)], wkv[pl.ds(0, 512), :])

        def add_kv(j, _):
            part_kv[...] += nn(sts[:, col(j, 512)], wkv[col(j, 512), :])
            return _

        lax.fori_loop(1, 7, add_kv, 0)
        push("exk", part_kv.at[:, head_o], other_kv.at[0], to_sib)
        push("exk", part_kv.at[:, head_vo], other_kv.at[1], to_sib)

    def queries():
        wait(*q_all)
        part[0] = nn(anc[0], wq[0])

        def add_q(k, _):
            part[0] += nn(anc[k], wq[k])
            return _

        lax.fori_loop(1, NS, add_q, 0)
        push("exq", part.at[0, :, head_o], other.at[0], to_sib)

    factor = HEAD ** (-0.5)
    block = 128

    def attend(r):
        def run():
            if r == 0:
                wait("exk")
                k_h[...] = (part_kv[:, head] + other_kv[0]).astype(BF)
                v_h[...] = (part_kv[:, head_v] + other_kv[1]).astype(BF)
                wait("exq")
                q_h[...] = (part[0, :, head] + other[0]).astype(BF)
            rows = pl.ds(r * block, block)
            scores = nt(q_h[rows, :], k_h[...]) * factor
            reach = lax.broadcasted_iota(jnp.int32, (block, LEN), 0) + (r * block + lag[0])
            allowed = lax.broadcasted_iota(jnp.int32, (block, LEN), 1) <= reach
            scores = jnp.where(allowed, scores, -jnp.inf)
            expo = jnp.exp(scores - jnp.max(scores, axis=1, keepdims=True))
            p = expo / jnp.sum(expo, axis=1, keepdims=True)
            probs[rows, :] = p
            a = p.astype(BF)
            att[rows, :] = a
            ctx[rows, head] = nn(a, v_h[...]).astype(BF)
            if r == LEN // block - 1:
                push("ectx", ctx.at[:, head], ctx.at[:, head], to_sib)
        return run

    tasks["kv"] = keys_values
    tasks["q"] = queries
    for r in range(LEN // block):
        tasks["attn%d" % r] = attend(r)

    def back_context():
        wait(*o_all)
        wait(*z_all)
        part[1] = nt(cot[0], wo[0])

        def add_b(k, _):
            part[1] += nt(cot[k], wo[k])
            return _

        lax.fori_loop(1, NS, add_b, 0)
        push("eb", part.at[1, :, head_o], other.at[1], to_sib)

    tasks["bc"] = back_context

    def backward(r):
        def run():
            if r == 0:
                wait("eb")
                b_h[...] = (part[1, :, head] + other[1]).astype(BF)
            rows = pl.ds(r * block, block)
            dprobs = nt(b_h[rows, :], v_h[...])
            delta = jnp.sum(b_h[rows, :].astype(F32) * ctx[rows, head].astype(F32), axis=1, keepdims=True)
            ds = (probs[rows, :] * (dprobs - delta) * factor).astype(BF)
            qb[rows, head] = nn(ds, k_h[...]).astype(BF)
            kt = tn(ds, q_h[rows, :])
            vt = tn(att[rows, :], b_h[rows, :])
            if r == 0:
                other_kv[0] = kt
                other_kv[1] = vt
            else:
                other_kv[0] += kt
                other_kv[1] += vt
            if r == LEN // block - 1:
                kvb[:, head] = other_kv[0].astype(BF)
                kvb[:, head_v] = other_kv[1].astype(BF)
                push("ekb", kvb.at[:, head], kvb.at[:, head], to_sib)
                push("ekb", kvb.at[:, head_v], kvb.at[:, head_v], to_sib)
                push("ekb", qb.at[:, head], qb.at[:, head], to_sib)
        return run

    for r in range(LEN // block):
        tasks["bwd%d" % r] = backward(r)

    def slot(off, j):
        k = (dp + 2 * off + NS) % NS
        return flip(k) if j else k

    def add(s, k, rows, got):
        s[k, rows] = (s[k, rows].astype(F32) + got.astype(F32)).astype(BF)

    def sum_x_first(name, ready, s, r0, n, ra, rc, ry, make, out):
        h = n // 2
        lo, hi = pl.ds(r0, h), pl.ds(r0 + h, h)
        full = pl.ds(r0, n)

        def first(j):
            def run():
                ready()
                k = slot(2, j)
                make(k, r0, n)
                push(name + "a%d" % j, s.at[k, lo], ra.at[0, j], to_xr)
                push(name + "a%d" % j, s.at[k, hi], ra.at[1, j], to_xl)
            return run

        def second(j):
            def run():
                k, m = slot(1, j), slot(-1, j)
                make(k, r0, n)
                push(name + "b%d" % j, s.at[k, hi], rc.at[0, j, pl.ds(h, h)], to_xr)
                make(m, r0, n)
                push(name + "b%d" % j, s.at[m, lo], rc.at[1, j, pl.ds(0, h)], to_xl)
            return run

        def own():
            make(slot(0, 1), r0, n)
            make(slot(0, 0), r0, n)

        def on(j):
            def run():
                wait(name + "a%d" % j)
                k, m = slot(1, j), slot(-1, j)
                add(s, k, lo, ra[0, j])
                push(name + "p%d" % j, s.at[k, lo], rc.at[0, j, pl.ds(0, h)], to_xr)
                add(s, m, hi, ra[1, j])
                push(name + "p%d" % j, s.at[m, hi], rc.at[1, j, pl.ds(h, h)], to_xl)
            return run

        def total(j):
            wait(name + "b%d" % j, name + "p%d" % j)
            return s[slot(0, j), full].astype(F32) + rc[0, j].astype(F32) + rc[1, j].astype(F32)

        def across():
            k = slot(0, 1)
            s[k, full] = total(1).astype(BF)
            push(name + "y", s.at[k, full], ry, to_yp)

        def finish():
            both = total(0)
            wait(name + "y")
            out(both + ry[...].astype(F32), r0, n)

        for j in (0, 1):
            tasks[name + ".a%d" % j] = first(j)
            tasks[name + ".b%d" % j] = second(j)
            tasks[name + ".p%d" % j] = on(j)
        tasks[name + ".m0"] = own
        tasks[name + ".y"] = across
        tasks[name + ".f"] = finish

    def sum_y_first(name, ready, s, r0, n, ra, rc, ry, make, out):
        h = n // 2
        lo, hi = pl.ds(r0, h), pl.ds(r0 + h, h)
        full = pl.ds(r0, n)
        offs = (2, 1, -1, 0)

        def first(i):
            def run():
                ready()
                k = slot(offs[i], 1)
                make(k, r0, n)
                push(name + "y%d" % i, s.at[k, full], ry.at[i], to_yp)
            return run

        def own():
            for off in offs:
                make(slot(off, 0), r0, n)

        def from_y():
            wait(name + "y0")
            k = slot(2, 0)
            add(s, k, full, ry[0])
            push(name + "a", s.at[k, lo], ra.at[0], to_xr)
            push(name + "a_", s.at[k, hi], ra.at[1], to_xl)

        def right():
            wait(name + "y1")
            k = slot(1, 0)
            add(s, k, full, ry[1])
            push(name + "b", s.at[k, hi], rc.at[0, pl.ds(h, h)], to_xr)

        def left():
            wait(name + "y2")
            m = slot(-1, 0)
            add(s, m, full, ry[2])
            push(name + "b", s.at[m, lo], rc.at[1, pl.ds(0, h)], to_xl)

        def on_right():
            wait(name + "a")
            k = slot(1, 0)
            add(s, k, lo, ra[0])
            push(name + "p", s.at[k, lo], rc.at[0, pl.ds(0, h)], to_xr)

        def on_left():
            wait(name + "a_")
            m = slot(-1, 0)
            add(s, m, hi, ra[1])
            push(name + "p", s.at[m, hi], rc.at[1, pl.ds(h, h)], to_xl)

        def finish():
            wait(name + "y3", name + "b", name + "p")
            k = slot(0, 0)
            out(s[k, full].astype(F32) + ry[3].astype(F32) + rc[0].astype(F32) + rc[1].astype(F32), r0, n)

        for i in range(4):
            tasks[name + ".y%d" % i] = first(i)
        tasks[name + ".m"] = own
        tasks[name + ".a"] = from_y
        tasks[name + ".b"] = right
        tasks[name + ".b_"] = left
        tasks[name + ".p"] = on_right
        tasks[name + ".p_"] = on_left
        tasks[name + ".f"] = finish

    def make_out(k, r0, n):
        s_out[k, pl.ds(r0, n)] = tn(ctx[:, pl.ds(r0, n)], cot[k]).astype(BF)

    def put_out(total, r0, n):
        g_out[pl.ds(r0, n)] = total.astype(BF)

    def make_kv(k, r0, n):
        s_kv[k] = nn(sts_t[pl.ds(pl.multiple_of((2 * k + c) * 224, 224), 224), :], kvb[...]).astype(BF)

    def put_kv(total, r0, n):
        g_key[...] = total[:, :256].astype(BF)
        g_value[...] = total[:, 256:].astype(BF)

    def make_q(k, r0, n):
        s_q[k, pl.ds(r0, n)] = nn(anc_t[k, pl.ds(r0, n), :], qb[...]).astype(BF)

    def put_q(total, r0, n):
        g_query[pl.ds(r0, n)] = total.astype(BF)

    def ctx_ready():
        wait(*z_all)
        wait("ectx")

    def back_ready():
        wait("ekb")

    ra_oa, ra_ob = ra_out
    rc_oa, rc_ob = rc_out
    ry_oa, ry_ob = ry_out
    ra_qa, ra_qb = ra_q
    rc_qa, rc_qb = rc_q
    ry_qa, ry_qb = ry_q
    if GO_Y:
        sum_y_first("goA", ctx_ready, s_out, 0, GO_Y, ra_oa, rc_oa, ry_oa, make_out, put_out)
    if GO_Y < 256:
        sum_x_first("goB", ctx_ready, s_out, GO_Y, 256 - GO_Y, ra_ob, rc_ob, ry_ob, make_out, put_out)
    sum_x_first("gkv", back_ready, s_kv, 0, 224, ra_kv, rc_kv, ry_kv, make_kv, put_kv)
    if GQ_Y:
        sum_y_first("gqA", back_ready, s_q, 0, GQ_Y, ra_qa, rc_qa, ry_qa, make_q, put_q)
    if GQ_Y < 512:
        sum_x_first("gqB", back_ready, s_q, GQ_Y, 512 - GQ_Y, ra_qb, rc_qb, ry_qb, make_q, put_q)

    def ring_add(step, part_):
        def run():
            a, b = (lo_tok, hi_tok) if part_ == "a" else (hi_tok, lo_tok)
            k, m = (z + 5 - step) % NS, (z + 3 + step) % NS
            if step > 1 and (step, part_) != (2, "b"):
                wait("U%d%s" % (step - 1, part_))
                add(upd, k, a, rz[0, step - 2, a])
                push("U%d%s" % (step, part_), upd.at[k, a], rz.at[0, step - 1, a], to_zr)
                add(upd, m, b, rz[1, step - 2, b])
                push("U%d%s" % (step, part_), upd.at[m, b], rz.at[1, step - 1, b], to_zl)
            else:
                push("U%d%s" % (step, part_), upd.at[k, a], rz.at[0, step - 1, a], to_zr)
                push("U%d%s" % (step, part_), upd.at[m, b], rz.at[1, step - 1, b], to_zl)
        return run

    def updates():
        wait("ectx")
        wait(*o_all)

        def make_upd(k, _):
            upd[k] = nn(ctx[...], wo[k]).astype(BF)
            return _

        lax.fori_loop(0, NS, make_upd, 0)
        ring_add(1, "a")()
        ring_add(2, "b")()

    tasks["upd"] = updates
    for step in (2, 3, 4):
        for part_ in ("a", "b"):
            if (step, part_) != (2, "b"):
                tasks["u%d%s" % (step, part_)] = ring_add(step, part_)

    given = upd.at[z, pl.ds(pl.multiple_of(o * TOK, TOK), TOK)]
    fin_own = pltpu.make_async_copy(upd.at[z, mine], ru.at[0], fin_recv.at[0])
    fin_sib = pltpu.make_async_remote_copy(
        src_ref=given, dst_ref=ru.at[0], send_sem=near_send.at[2], recv_sem=fin_recv.at[0],
        device_id=to_sib, device_id_type=MESH)
    fin_far = [
        pltpu.make_async_remote_copy(
            src_ref=upd.at[z, pl.ds(h * TOK, TOK)], dst_ref=ru.at[1], send_sem=near_send.at[3 + h],
            recv_sem=fin_recv.at[1], device_id=(dp, h, ty), device_id_type=MESH)
        for h in (0, 1)
    ]

    def last_exchange():
        wait("U4a", "U4b")
        upd[z] = (upd[z].astype(F32) + rz[0, 3].astype(F32) + rz[1, 3].astype(F32)).astype(BF)

        @pl.when(same)
        def _():
            fin_own.start()
            fin_sib.start()

        @pl.when(jnp.logical_not(same))
        def _():
            fin_far[0].start()
            fin_far[1].start()

    def last_sum():
        for i in (0, 1):
            pltpu.make_async_copy(ru.at[i], ru.at[i], fin_recv.at[i]).wait()
        update[0] = (ru[0].astype(F32) + ru[1].astype(F32)).astype(BF)

    tasks["u5"] = last_exchange
    tasks["ufin"] = last_sum

    for name in ORDER:
        tasks.pop(name)()
    assert not tasks and not arriving

    for copy in started:
        copy.wait_send()
    cot_far.wait_send()

    @pl.when(jnp.logical_not(same))
    def _():
        cot_sib.wait_send()
        fin_far[0].wait_send()
        fin_far[1].wait_send()

    @pl.when(same)
    def _():
        fin_sib.wait_send()


def hand_on(*refs):
    copies = [pltpu.make_async_copy(refs[i], refs[5 + i], refs[10].at[i]) for i in range(5)]
    for copy in copies:
        copy.start()
    for copy in copies:
        copy.wait()


def local(*args):
    vm = pltpu.VMEM
    shapes = [
        ((1, TOK, 512), BF), ((512, 256), BF), ((224, 256), BF), ((224, 256), BF), ((256, 512), BF),
    ]

    def landing(n, width, cut):
        a, b = max(cut, 32), max(n - cut, 32)
        ra = [vm((2, a // 2, width), BF), vm((2, 2, b // 2, width), BF)]
        rc = [vm((2, a, width), BF), vm((2, 2, b, width), BF)]
        ry = [vm((4, a, width), BF), vm((b, width), BF)]
        return [ra, rc, ry]

    scratch = [
        vm((NS, LEN, 512), BF), vm((NS, 512, LEN), BF), vm((LEN, 3584), BF), vm((3584, LEN), BF),
        vm((NS, LEN, 512), BF), vm((NS, 512, 256), BF), vm((3584, 512), BF), vm((NS, 256, 512), BF),
        vm((NS, 256, 512), BF), vm((NS, 224, 512), BF), vm((NS, 512, 256), BF),
        vm((NS, LEN, 512), BF), vm((2, 4, LEN, 512), BF), vm((2, TOK, 512), BF),
        *landing(256, 512, GO_Y),
        vm((2, 2, 112, 512), BF), vm((2, 2, 224, 512), BF), vm((224, 512), BF),
        *landing(512, 256, GQ_Y),
        vm((2, LEN, 256), F32), vm((LEN, 512), F32), vm((2, LEN, HEAD), F32), vm((2, LEN, HEAD), F32),
        vm((LEN, HEAD), BF), vm((LEN, HEAD), BF), vm((LEN, HEAD), BF), vm((LEN, HEAD), BF),
        vm((LEN, LEN), F32), vm((LEN, LEN), BF), vm((LEN, 256), BF), vm((LEN, 256), BF), vm((LEN, 512), BF),
        pltpu.SMEM((1,), jnp.int32), vm((TOK, 512), BF),
        pltpu.SemaphoreType.DMA((COPIES,)), pltpu.SemaphoreType.DMA((COPIES,)),
        pltpu.SemaphoreType.DMA((5,)), pltpu.SemaphoreType.DMA((2,)), pltpu.SemaphoreType.DMA((2,)),
        pltpu.SemaphoreType.DMA((16,)),
    ]
    any_ = pl.BlockSpec(memory_space=pl.ANY)
    vmem = pl.BlockSpec(memory_space=pltpu.VMEM)
    results = [jax.ShapeDtypeStruct(s, d) for s, d in shapes]
    outs = pl.pallas_call(
        kernel,
        out_shape=[pltpu.VMEM(s, d) for s, d in shapes],
        in_specs=[any_, any_, pl.BlockSpec(memory_space=pltpu.HBM)] + [any_] * 5,
        out_specs=[vmem] * 5,
        scratch_shapes=scratch,
        compiler_params=pltpu.CompilerParams(
            collective_id=0, has_side_effects=True, vmem_limit_bytes=56 * 2**20
        ),
        name="block",
    )(*args)
    outs = [pltpu.with_memory_space_constraint(out, pltpu.VMEM) for out in outs]
    return pl.pallas_call(
        hand_on,
        out_shape=results,
        in_specs=[vmem] * 5,
        out_specs=[any_] * 5,
        scratch_shapes=[pltpu.SemaphoreType.DMA((5,))],
        name="hand_on",
    )(*outs)


def solution(mesh):
    placed = (
        P("dp", "seq", None),
        P("dp", "seq", None),
        P("dp"),
        P(("dp", "seq"), "tensor"),
        P(("dp", "seq"), "tensor"),
        P(("dp", "seq"), "tensor"),
        P("tensor", ("dp", "seq")),
        P("dp", "seq", "tensor"),
    )
    return jax.shard_map(
        local,
        mesh=mesh,
        in_specs=placed,
        out_specs=(
            P("dp", "seq", "tensor"),
            P(("dp", "seq"), "tensor"),
            P(("dp", "seq"), "tensor"),
            P(("dp", "seq"), "tensor"),
            P("tensor", ("dp", "seq")),
        ),
        check_vma=False,
    )
```

```python
import jax
import jax.numpy as jnp
from jax import lax
from jax.experimental import pallas as pl
from jax.experimental.pallas import tpu as pltpu
from jax.sharding import PartitionSpec as P

MESH = pl.DeviceIdType.MESH
BF = jnp.bfloat16
F32 = jnp.float32
HEAD = 128
TOK = 192
LEN = 384
NS = 8
COPIES = 256

Q_Y, O_Y, GQ_Y, GO_Y = 320, 128, 192, 96

FIRST = ('kv', 'qB', 'qA')
O_LAST_Y = 0

ORDER = (
    "z1a", "z1b", "kv.fx", "qB.fx", "kv.fy", "qA.fx", "z2a", "qB.fy", "turn0", "turn1", "turn2", "turn3",
    "turn4", "turn5", "q0", "z2b", "turn6", "turn7", "e0", "kv.fxf", "z3a", "own_o", "qA.fxf", "qB.fxf",
    "z3b", "e1", "kv", "z4a", "oA.fx", "oB.fy", "oB.fx", "q", "oA.fxf", "e2", "attn0", "oB.fxf", "attn1",
    "attn2", "e3", "goB.a0", "goB.a1", "goB.b0", "upd", "upd2", "goB.b1", "goA.y0", "goA.y1", "goA.y2",
    "goA.y3", "bc", "e4", "goB.m0", "goA.m", "goB.p0", "goB.p1", "bwd0", "u2a", "bwd1", "bwd2", "goA.a",
    "goA.b", "u3b", "goA.b_", "goB.y", "gqB.a0", "gqB.a1", "gqB.b0", "gqB.b1", "goA.p", "goA.p_", "gqA.y0",
    "gqA.y1", "gqA.y2", "gqA.y3", "gqB.m0", "gqA.m", "u3a", "kvf", "gqB.p0", "gqB.p1", "gkv.a", "gkv.b",
    "goB.f", "gkv.m", "u4b", "gqA.a", "goA.f", "gqA.b", "u4a", "gqA.b_", "gqB.y", "gkv.p", "u5", "gqA.p",
    "gqA.p_", "gqB.f", "u6", "gkv.f", "gqA.f", "ufin",
)


def nn(a, b):
    return jnp.dot(a, b, preferred_element_type=F32)


def nt(a, b):
    return lax.dot_general(a, b, (((1,), (1,)), ((), ())), preferred_element_type=F32)


def tn(a, b):
    return lax.dot_general(a, b, (((0,), (0,)), ((), ())), preferred_element_type=F32)


def kernel(
    anchor, augment, lag_in, w_query, w_key, w_value, w_out, cot_in,
    update, g_query, g_key, g_value, g_out,
    anc, anc_t, sts, sts_t, cot, wq, wkv, wo,
    s_out, s_kv, s_q, upd, rz, ru,
    ra_out, rc_out, ry_out, ra_kv, rc_kv, sts_y, kvb_y, ra_q, rc_q, ry_q,
    part, part_kv, other, other_kv, q_h, k_h, v_h, b_h, probs, att, ctx, qb, kvb,
    lag, stage,
    send, recv, near_send, near_recv, fin_recv, local,
):
    dp, c, t = lax.axis_index("dp"), lax.axis_index("seq"), lax.axis_index("tensor")
    z, yl = t // 2, t % 2
    o = 1 - c
    xr, xl = (dp + 2) % NS, (dp + 6) % NS
    far = (dp + 4) % NS
    yp = dp + 1 - 2 * (dp % 2)
    ty = t + 1 - 2 * yl
    to_xr, to_xl, to_yp = (xr, c, t), (xl, c, t), (yp, c, t)
    to_zr, to_zl = (dp, c, (t + 2) % 16), (dp, c, (t + 14) % 16)
    to_sib = (dp, o, t)
    same = c == yl

    barrier = pltpu.get_barrier_semaphore()
    partners = (to_xr, to_xl, to_yp, to_zr, to_zl, to_sib, (dp, 0, ty), (dp, 1, ty))
    for who in partners:
        pl.semaphore_signal(barrier, inc=1, device_id=who, device_id_type=MESH)

    started = []
    arriving = {}
    tasks = {}

    def push(name, src, dst, who):
        i = len(started)
        copy = pltpu.make_async_remote_copy(
            src_ref=src, dst_ref=dst, send_sem=send.at[i], recv_sem=recv.at[i],
            device_id=who, device_id_type=MESH,
        )
        copy.start()
        started.append(copy)
        arriving.setdefault(name, []).append(copy)

    def wait(*names):
        for name in names:
            for copy in arriving.pop(name, ()):
                copy.wait_recv()

    locals_ = []

    def fetch(src, dst):
        copy = pltpu.make_async_copy(src, dst, local.at[len(locals_)])
        copy.start()
        locals_.append(copy)

    def col(i, n):
        return pl.ds(pl.multiple_of(i * n, n), n)

    def flip(k):
        return k + 1 - 2 * (k % 2)

    mine = pl.ds(pl.multiple_of(c * TOK, TOK), TOK)
    head = col(c, HEAD)
    head_o = col(o, HEAD)
    head_v = pl.ds(pl.multiple_of(256 + c * HEAD, HEAD), HEAD)
    head_vo = pl.ds(pl.multiple_of(256 + o * HEAD, HEAD), HEAD)

    def kv_rows(k, r0, n):
        return pl.ds(pl.multiple_of((2 * k + c) * 224 + r0, 16), n)

    def rows_of(buf):
        return lambda k, r0, n: buf.at[k, pl.ds(r0, n)]

    def slot_kv(k, r0, n):
        return wkv.at[kv_rows(k, r0, n)]

    def y_first(name, slot, r0, n):
        h = n // 2
        mine_ = slot(dp, r0, n)

        def from_y():
            wait(name + "y")
            s = slot(yp, r0, n)
            push(name + "fr", s, s, to_xr)
            push(name + "fl", s, s, to_xl)

        def near(first, second, a, b):
            def run():
                wait(name + first + "r", name + first + "l")
                lo, hi = slot(a, r0, h), slot(b, r0 + h, h)
                push(name + second + "0", lo, lo, to_xr)
                push(name + second + "1", hi, hi, to_xl)
            return run

        tasks[name + ".fy"] = from_y
        tasks[name + ".fx"] = near("", "h", xl, xr)
        tasks[name + ".fxf"] = near("f", "g", flip(xl), flip(xr))
        push(name + "y", mine_, mine_, to_yp)
        push(name + "r", mine_, mine_, to_xr)
        push(name + "l", mine_, mine_, to_xl)
        return [name + e for e in ("y", "r", "l", "fr", "fl", "h0", "h1", "g0", "g1")]

    def x_first(name, slot, r0, n):
        h = n // 2
        mine_ = slot(dp, r0, n)

        def from_x():
            wait(name + "r", name + "l")
            lo, hi = slot(xl, r0, h), slot(xr, r0 + h, h)
            push(name + "h0", lo, lo, to_xr)
            push(name + "h1", hi, hi, to_xl)
            a, b = slot(xl, r0, n), slot(xr, r0, n)
            push(name + "y0", a, a, to_yp)
            push(name + "y1", b, b, to_yp)

        def from_far():
            for i in (0, 1):
                wait(name + "h%d" % i)
                s = slot(far, r0 + i * h, h)
                push(name + "g%d" % i, s, s, to_yp)

        tasks[name + ".fx"] = from_x
        tasks[name + ".fxf"] = from_far
        push(name + "r", mine_, mine_, to_xr)
        push(name + "l", mine_, mine_, to_xl)
        push(name + "y", mine_, mine_, to_yp)
        return [name + e for e in ("y", "r", "l", "h0", "h1", "y0", "y1", "g0", "g1")]

    own_kv = kv_rows(dp, 0, 224)
    fetch(cot_in.at[0], stage)
    fetch(w_key, wkv.at[own_kv, pl.ds(0, 256)])
    fetch(w_value, wkv.at[own_kv, pl.ds(256, 256)])
    fetch(w_query, wq.at[dp])
    fetch(w_out, wo.at[dp])
    early = len(locals_)
    fetch(lag_in, lag)
    for copy in locals_[:early]:
        copy.wait()
    pl.semaphore_wait(barrier, len(partners))

    cot_dst = cot.at[z, mine]
    cot_far = pltpu.make_async_remote_copy(
        src_ref=stage, dst_ref=cot_dst, send_sem=near_send.at[0], recv_sem=near_recv.at[c],
        device_id=(dp, yl, ty), device_id_type=MESH)
    cot_sib = pltpu.make_async_remote_copy(
        src_ref=stage, dst_ref=cot_dst, send_sem=near_send.at[1], recv_sem=near_recv.at[c],
        device_id=to_sib, device_id_type=MESH)
    cot_own = pltpu.make_async_copy(stage, cot_dst, near_recv.at[c])
    cot_far.start()

    @pl.when(same)
    def _():
        cot_own.start()

    @pl.when(jnp.logical_not(same))
    def _():
        cot_sib.start()

    kv_all, q_all, o_all = [], [], []

    def gather_q_a():
        if Q_Y:
            q_all.extend(x_first("qA", rows_of(wq), 0, Q_Y))

    def gather_q_b():
        if Q_Y < 512:
            q_all.extend(y_first("qB", rows_of(wq), Q_Y, 512 - Q_Y))

    def gather_kv():
        kv_all.extend(y_first("kv", slot_kv, 0, 224))

    first = {"kv": gather_kv, "qA": gather_q_a, "qB": gather_q_b}
    for name in FIRST:
        first[name]()

    def gather_o_a():
        if O_Y:
            o_all.extend(x_first("oA", rows_of(wo), 0, O_Y))

    def gather_o_b():
        if O_Y < 256:
            o_all.extend(y_first("oB", rows_of(wo), O_Y, 256 - O_Y))

    def own_o():
        for run in (gather_o_b, gather_o_a) if O_LAST_Y else (gather_o_a, gather_o_b):
            run()

    tasks["own_o"] = own_o

    push("sib", augment.at[0], sts.at[mine], to_sib)
    fetch(augment.at[0], sts.at[mine])
    for k in range(NS):
        push("sib", anchor.at[0, :, pl.ds(pl.multiple_of((2 * k + o) * 512, 512), 512)], anc.at[k, mine], to_sib)
        fetch(anchor.at[0, :, pl.ds(pl.multiple_of((2 * k + c) * 512, 512), 512)], anc.at[k, mine])

    zero = jnp.zeros((224, 512), BF)
    for k in range(NS):
        wkv[pl.ds(pl.multiple_of((2 * k + o) * 224, 224), 224), :] = zero

    lo_tok, hi_tok = pl.ds(0, TOK), pl.ds(TOK, TOK)

    def ring(step, part_):
        def run():
            a, b = (lo_tok, hi_tok) if part_ == "a" else (hi_tok, lo_tok)
            if step == 1 and part_ == "a":
                for h in (0, 1):
                    got = cot.at[z, pl.ds(h * TOK, TOK)]
                    pltpu.make_async_copy(got, got, near_recv.at[h]).wait()
            if step > 1:
                wait("Z%d%s" % (step - 1, part_))
            s, r = cot.at[(z + 9 - step) % NS, a], cot.at[(z + step - 1) % NS, b]
            push("Z%d%s" % (step, part_), s, s, to_zr)
            push("Z%d%s" % (step, part_), r, r, to_zl)
        return run

    z_all = []
    for step in range(1, 5):
        for part_ in ("a", "b") if step < 4 else ("a",):
            tasks["z%d%s" % (step, part_)] = ring(step, part_)
            z_all.append("Z%d%s" % (step, part_))

    def turn(i):
        def run():
            if i == 0:
                wait("sib")
                for copy in locals_[early:]:
                    copy.wait()
            anc_t[i] = anc[i].T
            if i < 7:
                sts_t[pl.ds(i * 512, 512), :] = sts[:, pl.ds(i * 512, 512)].T
        return run

    for i in range(NS):
        tasks["turn%d" % i] = turn(i)

    def states_y():
        k = 2 * (z // 2) + 1 - dp % 2
        src = sts_t.at[pl.ds(pl.multiple_of((2 * k + c) * 224 + (z % 2) * 112, 112), 112)]
        push("E0", src, sts_y.at[pl.ds(pl.multiple_of(z * 112, 112), 112)], to_yp)

    def states_ring(step):
        def run():
            wait("E%d" % (step - 1))
            s = sts_y.at[pl.ds(pl.multiple_of(((z + 9 - step) % NS) * 112, 112), 112)]
            push("E%d" % step, s, s, to_zr)
            if step < 4:
                s = sts_y.at[pl.ds(pl.multiple_of(((z + step - 1) % NS) * 112, 112), 112)]
                push("E%d" % step, s, s, to_zl)
        return run

    tasks["e0"] = states_y
    for step in range(1, 5):
        tasks["e%d" % step] = states_ring(step)

    def keys_values():
        wait(*kv_all)
        part_kv[...] = nn(sts[:, pl.ds(0, 512)], wkv[pl.ds(0, 512), :])

        def add_kv(j, _):
            part_kv[...] += nn(sts[:, col(j, 512)], wkv[col(j, 512), :])
            return _

        lax.fori_loop(1, 7, add_kv, 0)
        push("exk", part_kv.at[:, head_o], other_kv.at[0], to_sib)
        push("exk", part_kv.at[:, head_vo], other_kv.at[1], to_sib)

    def queries_near():
        wait("qAy", "qAr", "qAl", "qBy", "qBr", "qBl")
        part[0] = nn(anc[dp], wq[dp])
        for k in (yp, xl, xr):
            part[0] += nn(anc[k], wq[k])

    def queries():
        wait(*q_all)
        for k in (flip(xl), flip(xr), far, flip(far)):
            part[0] += nn(anc[k], wq[k])
        push("exq", part.at[0, :, head_o], other.at[0], to_sib)

    factor = HEAD ** (-0.5)
    block = 128

    def attend(r):
        def run():
            if r == 0:
                wait("exk")
                k_h[...] = (part_kv[:, head] + other_kv[0]).astype(BF)
                v_h[...] = (part_kv[:, head_v] + other_kv[1]).astype(BF)
                wait("exq")
                q_h[...] = (part[0, :, head] + other[0]).astype(BF)
            rows = pl.ds(r * block, block)
            scores = nt(q_h[rows, :], k_h[...]) * factor
            reach = lax.broadcasted_iota(jnp.int32, (block, LEN), 0) + (r * block + lag[0])
            allowed = lax.broadcasted_iota(jnp.int32, (block, LEN), 1) <= reach
            scores = jnp.where(allowed, scores, -jnp.inf)
            expo = jnp.exp(scores - jnp.max(scores, axis=1, keepdims=True))
            p = expo / jnp.sum(expo, axis=1, keepdims=True)
            probs[rows, :] = p
            a = p.astype(BF)
            att[rows, :] = a
            ctx[rows, head] = nn(a, v_h[...]).astype(BF)
            push("ectx%d" % r, ctx.at[rows, head], ctx.at[rows, head], to_sib)
        return run

    tasks["kv"] = keys_values
    tasks["q0"] = queries_near
    tasks["q"] = queries
    for r in range(LEN // block):
        tasks["attn%d" % r] = attend(r)

    def back_context():
        wait(*o_all)
        wait(*z_all)
        part[1] = nt(cot[0], wo[0])

        def add_b(k, _):
            part[1] += nt(cot[k], wo[k])
            return _

        lax.fori_loop(1, NS, add_b, 0)
        push("eb", part.at[1, :, head_o], other.at[1], to_sib)

    tasks["bc"] = back_context

    def backward(r):
        def run():
            if r == 0:
                wait("eb")
                b_h[...] = (part[1, :, head] + other[1]).astype(BF)
            rows = pl.ds(r * block, block)
            dprobs = nt(b_h[rows, :], v_h[...])
            delta = jnp.sum(b_h[rows, :].astype(F32) * ctx[rows, head].astype(F32), axis=1, keepdims=True)
            ds = (probs[rows, :] * (dprobs - delta) * factor).astype(BF)
            qb[rows, head] = nn(ds, k_h[...]).astype(BF)
            kt = tn(ds, q_h[rows, :])
            vt = tn(att[rows, :], b_h[rows, :])
            if r == 0:
                other_kv[0] = kt
                other_kv[1] = vt
            else:
                other_kv[0] += kt
                other_kv[1] += vt
            if r == LEN // block - 1:
                kvb[:, head] = other_kv[0].astype(BF)
                kvb[:, head_v] = other_kv[1].astype(BF)
                push("KX", kvb.at[:, head], kvb_y.at[:, head], to_yp)
                push("KX", kvb.at[:, head_v], kvb_y.at[:, head_v], to_yp)
                push("ekb", kvb.at[:, head], kvb.at[:, head], to_sib)
                push("ekb", kvb.at[:, head_v], kvb.at[:, head_v], to_sib)
                push("ekb", qb.at[:, head], qb.at[:, head], to_sib)
        return run

    for r in range(LEN // block):
        tasks["bwd%d" % r] = backward(r)

    def hand_over():
        wait("KX")
        push("KF", kvb_y.at[:, head], kvb_y.at[:, head], to_sib)
        push("KF", kvb_y.at[:, head_v], kvb_y.at[:, head_v], to_sib)

    tasks["kvf"] = hand_over

    def slot(off, j):
        k = (dp + 2 * off + NS) % NS
        return flip(k) if j else k

    def add(s, k, rows, got):
        s[k, rows] = (s[k, rows].astype(F32) + got.astype(F32)).astype(BF)

    def sum_x_first(name, ready, s, r0, n, ra, rc, ry, make, out):
        h = n // 2
        lo, hi = pl.ds(r0, h), pl.ds(r0 + h, h)
        full = pl.ds(r0, n)

        def first(j):
            def run():
                ready()
                k = slot(2, j)
                make(k, r0, n)
                push(name + "a%d" % j, s.at[k, lo], ra.at[0, j], to_xr)
                push(name + "a%d" % j, s.at[k, hi], ra.at[1, j], to_xl)
            return run

        def second(j):
            def run():
                k, m = slot(1, j), slot(-1, j)
                make(k, r0, n)
                push(name + "b%d" % j, s.at[k, hi], rc.at[0, j, pl.ds(h, h)], to_xr)
                make(m, r0, n)
                push(name + "b%d" % j, s.at[m, lo], rc.at[1, j, pl.ds(0, h)], to_xl)
            return run

        def own():
            make(slot(0, 1), r0, n)
            make(slot(0, 0), r0, n)

        def on(j):
            def run():
                wait(name + "a%d" % j)
                k, m = slot(1, j), slot(-1, j)
                add(s, k, lo, ra[0, j])
                push(name + "p%d" % j, s.at[k, lo], rc.at[0, j, pl.ds(0, h)], to_xr)
                add(s, m, hi, ra[1, j])
                push(name + "p%d" % j, s.at[m, hi], rc.at[1, j, pl.ds(h, h)], to_xl)
            return run

        def total(j):
            wait(name + "b%d" % j, name + "p%d" % j)
            return s[slot(0, j), full].astype(F32) + rc[0, j].astype(F32) + rc[1, j].astype(F32)

        def across():
            k = slot(0, 1)
            s[k, full] = total(1).astype(BF)
            push(name + "y", s.at[k, full], ry, to_yp)

        def finish():
            both = total(0)
            wait(name + "y")
            out(both + ry[...].astype(F32), r0, n)

        for j in (0, 1):
            tasks[name + ".a%d" % j] = first(j)
            tasks[name + ".b%d" % j] = second(j)
            tasks[name + ".p%d" % j] = on(j)
        tasks[name + ".m0"] = own
        tasks[name + ".y"] = across
        tasks[name + ".f"] = finish

    def sum_y_first(name, ready, s, r0, n, ra, rc, ry, make, out):
        h = n // 2
        lo, hi = pl.ds(r0, h), pl.ds(r0 + h, h)
        full = pl.ds(r0, n)
        offs = (2, 1, -1, 0)

        def first(i):
            def run():
                ready()
                k = slot(offs[i], 1)
                make(k, r0, n)
                push(name + "y%d" % i, s.at[k, full], ry.at[i], to_yp)
            return run

        def own():
            for off in offs:
                make(slot(off, 0), r0, n)

        def from_y():
            wait(name + "y0")
            k = slot(2, 0)
            add(s, k, full, ry[0])
            push(name + "a", s.at[k, lo], ra.at[0], to_xr)
            push(name + "a_", s.at[k, hi], ra.at[1], to_xl)

        def right():
            wait(name + "y1")
            k = slot(1, 0)
            add(s, k, full, ry[1])
            push(name + "b", s.at[k, hi], rc.at[0, pl.ds(h, h)], to_xr)

        def left():
            wait(name + "y2")
            m = slot(-1, 0)
            add(s, m, full, ry[2])
            push(name + "b", s.at[m, lo], rc.at[1, pl.ds(0, h)], to_xl)

        def on_right():
            wait(name + "a")
            k = slot(1, 0)
            add(s, k, lo, ra[0])
            push(name + "p", s.at[k, lo], rc.at[0, pl.ds(0, h)], to_xr)

        def on_left():
            wait(name + "a_")
            m = slot(-1, 0)
            add(s, m, hi, ra[1])
            push(name + "p", s.at[m, hi], rc.at[1, pl.ds(h, h)], to_xl)

        def finish():
            wait(name + "y3", name + "b", name + "p")
            k = slot(0, 0)
            out(s[k, full].astype(F32) + ry[3].astype(F32) + rc[0].astype(F32) + rc[1].astype(F32), r0, n)

        for i in range(4):
            tasks[name + ".y%d" % i] = first(i)
        tasks[name + ".m"] = own
        tasks[name + ".a"] = from_y
        tasks[name + ".b"] = right
        tasks[name + ".b_"] = left
        tasks[name + ".p"] = on_right
        tasks[name + ".p_"] = on_left
        tasks[name + ".f"] = finish

    def sum_x(name, ready, s, n, ra, rc, make, out):
        h = n // 2
        lo, hi = pl.ds(0, h), pl.ds(h, h)

        def first():
            ready()
            k = slot(2, 0)
            make(k, 0, n)
            push(name + "a", s.at[k, lo], ra.at[0], to_xr)
            push(name + "a", s.at[k, hi], ra.at[1], to_xl)

        def second():
            k, m = slot(1, 0), slot(-1, 0)
            make(k, 0, n)
            push(name + "b", s.at[k, hi], rc.at[0, hi], to_xr)
            make(m, 0, n)
            push(name + "b", s.at[m, lo], rc.at[1, lo], to_xl)

        def own():
            make(slot(0, 0), 0, n)

        def on():
            wait(name + "a")
            k, m = slot(1, 0), slot(-1, 0)
            add(s, k, lo, ra[0])
            push(name + "p", s.at[k, lo], rc.at[0, lo], to_xr)
            add(s, m, hi, ra[1])
            push(name + "p", s.at[m, hi], rc.at[1, hi], to_xl)

        def finish():
            wait(name + "b", name + "p")
            out(s[slot(0, 0)].astype(F32) + rc[0].astype(F32) + rc[1].astype(F32), 0, n)

        tasks[name + ".a"] = first
        tasks[name + ".b"] = second
        tasks[name + ".m"] = own
        tasks[name + ".p"] = on
        tasks[name + ".f"] = finish

    def make_out(k, r0, n):
        s_out[k, pl.ds(r0, n)] = tn(ctx[:, pl.ds(r0, n)], cot[k]).astype(BF)

    def put_out(total, r0, n):
        g_out[pl.ds(r0, n)] = total.astype(BF)

    def make_kv(k, r0, n):
        own_ = nn(sts_t[pl.ds(pl.multiple_of((2 * k + c) * 224, 224), 224), :], kvb[...])
        s_kv[k] = (own_ + nn(sts_y[pl.ds(pl.multiple_of((k // 2) * 224, 224), 224), :], kvb_y[...])).astype(BF)

    def put_kv(total, r0, n):
        g_key[...] = total[:, :256].astype(BF)
        g_value[...] = total[:, 256:].astype(BF)

    def make_q(k, r0, n):
        s_q[k, pl.ds(r0, n)] = nn(anc_t[k, pl.ds(r0, n), :], qb[...]).astype(BF)

    def put_q(total, r0, n):
        g_query[pl.ds(r0, n)] = total.astype(BF)

    ctx_all = ["ectx%d" % r for r in range(LEN // block)]

    def ctx_ready():
        wait(*z_all)
        wait(*ctx_all)

    def back_ready():
        wait("ekb")

    def both_ready():
        wait("ekb", "KF", "E1", "E2", "E3", "E4")

    ra_oa, ra_ob = ra_out
    rc_oa, rc_ob = rc_out
    ry_oa, ry_ob = ry_out
    ra_qa, ra_qb = ra_q
    rc_qa, rc_qb = rc_q
    ry_qa, ry_qb = ry_q
    if GO_Y:
        sum_y_first("goA", ctx_ready, s_out, 0, GO_Y, ra_oa, rc_oa, ry_oa, make_out, put_out)
    if GO_Y < 256:
        sum_x_first("goB", ctx_ready, s_out, GO_Y, 256 - GO_Y, ra_ob, rc_ob, ry_ob, make_out, put_out)
    sum_x("gkv", both_ready, s_kv, 224, ra_kv, rc_kv, make_kv, put_kv)
    if GQ_Y:
        sum_y_first("gqA", back_ready, s_q, 0, GQ_Y, ra_qa, rc_qa, ry_qa, make_q, put_q)
    if GQ_Y < 512:
        sum_x_first("gqB", back_ready, s_q, GQ_Y, 512 - GQ_Y, ra_qb, rc_qb, ry_qb, make_q, put_q)

    def ring_add(step, part_):
        def run():
            a, b = (lo_tok, hi_tok) if part_ == "a" else (hi_tok, lo_tok)
            k, m = (z + 5 - step) % NS, (z + 3 + step) % NS
            if step > 1 and (step, part_) != (2, "b"):
                wait("U%d%s" % (step - 1, part_))
                add(upd, k, a, rz[0, step - 2, a])
                add(upd, m, b, rz[1, step - 2, b])
            if (step, part_) == (4, "a"):
                for i, name in enumerate(("U4a", "U4c")):
                    first_, second_ = pl.ds(i * 96, 96), pl.ds(TOK + i * 96, 96)
                    push(name, upd.at[k, first_], rz.at[0, 3, first_], to_zr)
                    push(name, upd.at[m, second_], rz.at[1, 3, second_], to_zl)
            else:
                push("U%d%s" % (step, part_), upd.at[k, a], rz.at[0, step - 1, a], to_zr)
                push("U%d%s" % (step, part_), upd.at[m, b], rz.at[1, step - 1, b], to_zl)
        return run

    def make_upd(off):
        k = (z + off) % NS
        upd[k] = nn(ctx[...], wo[k]).astype(BF)

    def updates_far():
        wait(*ctx_all)
        wait(*o_all)
        for off in (4, 3, 5):
            make_upd(off)
        ring_add(1, "a")()
        ring_add(2, "b")()

    def updates():
        for off in (2, 6, 1, 7, 0):
            make_upd(off)

    tasks["upd"] = updates_far
    tasks["upd2"] = updates
    for step in (2, 3, 4):
        for part_ in ("a", "b"):
            if (step, part_) != (2, "b"):
                tasks["u%d%s" % (step, part_)] = ring_add(step, part_)

    def last_copies(i):
        rows = pl.ds(i * 96, 96)

        def half(h):
            return upd.at[z, pl.ds(pl.multiple_of(h * TOK + i * 96, 96), 96)]

        own_ = pltpu.make_async_copy(half(c), ru.at[0, rows], fin_recv.at[2 * i])
        sib_ = pltpu.make_async_remote_copy(
            src_ref=half(o), dst_ref=ru.at[0, rows], send_sem=near_send.at[2 + 3 * i], recv_sem=fin_recv.at[2 * i],
            device_id=to_sib, device_id_type=MESH)
        far_ = [
            pltpu.make_async_remote_copy(
                src_ref=half(h), dst_ref=ru.at[1, rows], send_sem=near_send.at[3 + 3 * i + h],
                recv_sem=fin_recv.at[2 * i + 1], device_id=(dp, h, ty), device_id_type=MESH)
            for h in (0, 1)
        ]
        return own_, sib_, far_

    last = [last_copies(i) for i in (0, 1)]

    def last_exchange(i):
        def run():
            if i == 0:
                wait("U4a", "U4b")
            else:
                wait("U4c")
            for h in (0, 1):
                rows = pl.ds(h * TOK + i * 96, 96)
                upd[z, rows] = (
                    upd[z, rows].astype(F32) + rz[0, 3, rows].astype(F32) + rz[1, 3, rows].astype(F32)
                ).astype(BF)
            own_, sib_, far_ = last[i]

            @pl.when(same)
            def _():
                own_.start()
                sib_.start()

            @pl.when(jnp.logical_not(same))
            def _():
                far_[0].start()
                far_[1].start()
        return run

    def last_sum():
        for i in (0, 1):
            rows = pl.ds(i * 96, 96)
            for j in (0, 1):
                pltpu.make_async_copy(ru.at[j, rows], ru.at[j, rows], fin_recv.at[2 * i + j]).wait()
        update[0] = (ru[0].astype(F32) + ru[1].astype(F32)).astype(BF)

    tasks["u5"] = last_exchange(0)
    tasks["u6"] = last_exchange(1)
    tasks["ufin"] = last_sum

    for name in ORDER:
        tasks.pop(name)()
    assert not tasks and not arriving

    for copy in started:
        copy.wait_send()
    cot_far.wait_send()

    @pl.when(jnp.logical_not(same))
    def _():
        cot_sib.wait_send()
        for _, _, far_ in last:
            far_[0].wait_send()
            far_[1].wait_send()

    @pl.when(same)
    def _():
        for _, sib_, _ in last:
            sib_.wait_send()


def hand_on(*refs):
    copies = [pltpu.make_async_copy(refs[i], refs[5 + i], refs[10].at[i]) for i in range(5)]
    for copy in copies:
        copy.start()
    for copy in copies:
        copy.wait()


def local(*args):
    vm = pltpu.VMEM
    shapes = [
        ((1, TOK, 512), BF), ((512, 256), BF), ((224, 256), BF), ((224, 256), BF), ((256, 512), BF),
    ]

    def landing(n, width, cut):
        a, b = max(cut, 32), max(n - cut, 32)
        ra = [vm((2, a // 2, width), BF), vm((2, 2, b // 2, width), BF)]
        rc = [vm((2, a, width), BF), vm((2, 2, b, width), BF)]
        ry = [vm((4, a, width), BF), vm((b, width), BF)]
        return [ra, rc, ry]

    scratch = [
        vm((NS, LEN, 512), BF), vm((NS, 512, LEN), BF), vm((LEN, 3584), BF), vm((3584, LEN), BF),
        vm((NS, LEN, 512), BF), vm((NS, 512, 256), BF), vm((3584, 512), BF), vm((NS, 256, 512), BF),
        vm((NS, 256, 512), BF), vm((NS, 224, 512), BF), vm((NS, 512, 256), BF),
        vm((NS, LEN, 512), BF), vm((2, 4, LEN, 512), BF), vm((2, TOK, 512), BF),
        *landing(256, 512, GO_Y),
        vm((2, 112, 512), BF), vm((2, 224, 512), BF), vm((896, LEN), BF), vm((LEN, 512), BF),
        *landing(512, 256, GQ_Y),
        vm((2, LEN, 256), F32), vm((LEN, 512), F32), vm((2, LEN, HEAD), F32), vm((2, LEN, HEAD), F32),
        vm((LEN, HEAD), BF), vm((LEN, HEAD), BF), vm((LEN, HEAD), BF), vm((LEN, HEAD), BF),
        vm((LEN, LEN), F32), vm((LEN, LEN), BF), vm((LEN, 256), BF), vm((LEN, 256), BF), vm((LEN, 512), BF),
        pltpu.SMEM((1,), jnp.int32), vm((TOK, 512), BF),
        pltpu.SemaphoreType.DMA((COPIES,)), pltpu.SemaphoreType.DMA((COPIES,)),
        pltpu.SemaphoreType.DMA((8,)), pltpu.SemaphoreType.DMA((2,)), pltpu.SemaphoreType.DMA((4,)),
        pltpu.SemaphoreType.DMA((16,)),
    ]
    any_ = pl.BlockSpec(memory_space=pl.ANY)
    vmem = pl.BlockSpec(memory_space=pltpu.VMEM)
    results = [jax.ShapeDtypeStruct(s, d) for s, d in shapes]
    outs = pl.pallas_call(
        kernel,
        out_shape=[pltpu.VMEM(s, d) for s, d in shapes],
        in_specs=[any_, any_, pl.BlockSpec(memory_space=pltpu.HBM)] + [any_] * 5,
        out_specs=[vmem] * 5,
        scratch_shapes=scratch,
        compiler_params=pltpu.CompilerParams(
            collective_id=0, has_side_effects=True, vmem_limit_bytes=56 * 2**20
        ),
        name="block",
    )(*args)
    outs = [pltpu.with_memory_space_constraint(out, pltpu.VMEM) for out in outs]
    return pl.pallas_call(
        hand_on,
        out_shape=results,
        in_specs=[vmem] * 5,
        out_specs=[any_] * 5,
        scratch_shapes=[pltpu.SemaphoreType.DMA((5,))],
        name="hand_on",
    )(*outs)


def solution(mesh):
    placed = (
        P("dp", "seq", None),
        P("dp", "seq", None),
        P("dp"),
        P(("dp", "seq"), "tensor"),
        P(("dp", "seq"), "tensor"),
        P(("dp", "seq"), "tensor"),
        P("tensor", ("dp", "seq")),
        P("dp", "seq", "tensor"),
    )
    return jax.shard_map(
        local,
        mesh=mesh,
        in_specs=placed,
        out_specs=(
            P("dp", "seq", "tensor"),
            P(("dp", "seq"), "tensor"),
            P(("dp", "seq"), "tensor"),
            P(("dp", "seq"), "tensor"),
            P("tensor", ("dp", "seq")),
        ),
        check_vma=False,
    )
```

```python
import jax
import jax.numpy as jnp
from jax import lax
from jax.experimental import pallas as pl
from jax.experimental.pallas import tpu as pltpu
from jax.sharding import PartitionSpec as P

MESH = pl.DeviceIdType.MESH
BF = jnp.bfloat16
F32 = jnp.float32
HEAD = 128
TOK = 192
LEN = 384
NS = 8
COPIES = 256

Q_Y, O_Y, GQ_Y, GO_Y = 288, 128, 256, 96

FIRST = ('kv', 'qB', 'qA')
O_LAST_Y = bool(0)

ORDER = (
    14, 15, 1, 21, 6, 22, 23, 24, 0, 25, 26, 3, 27, 16, 28, 5, 29, 35, 17, 2, 18, 13, 4, 30, 7, 19, 34, 20, 8,
    10, 31, 11, 36, 9, 37, 38, 12, 39, 32, 56, 59, 57, 60, 45, 90, 91, 40, 46, 47, 48, 33, 62, 49, 58, 50, 41,
    61, 42, 92, 43, 51, 52, 94, 53, 54, 70, 71, 72, 73, 63, 81, 84, 82, 85, 74, 87, 55, 44, 83, 93, 86, 65,
    66, 75, 67, 96, 76, 88, 77, 95, 68, 78, 79, 64, 97, 98, 89, 69, 80, 99,
)


def nn(a, b):
    return jnp.dot(a, b, preferred_element_type=F32)


def nt(a, b):
    return lax.dot_general(a, b, (((1,), (1,)), ((), ())), preferred_element_type=F32)


def tn(a, b):
    return lax.dot_general(a, b, (((0,), (0,)), ((), ())), preferred_element_type=F32)


def kernel(
    anchor, augment, lag_in, w_query, w_key, w_value, w_out, cot_in,
    update, g_query, g_key, g_value, g_out,
    anc, anc_t, sts, sts_t, cot, wq, wkv, wo,
    s_out, s_kv, s_q, upd, rz, ru,
    ra_out, rc_out, ry_out, ra_kv, rc_kv, sts_y, kvb_y, ra_q, rc_q, ry_q,
    part, part_kv, other, other_kv, q_h, k_h, v_h, b_h, probs, att, ctx, qb, kvb,
    lag, stage,
    send, recv, near_send, near_recv, fin_recv, local,
):
    dp, c, t = lax.axis_index("dp"), lax.axis_index("seq"), lax.axis_index("tensor")
    z, yl = t // 2, t % 2
    o = 1 - c
    xr, xl = (dp + 2) % NS, (dp + 6) % NS
    far = (dp + 4) % NS
    yp = dp + 1 - 2 * (dp % 2)
    ty = t + 1 - 2 * yl
    to_xr, to_xl, to_yp = (xr, c, t), (xl, c, t), (yp, c, t)
    to_zr, to_zl = (dp, c, (t + 2) % 16), (dp, c, (t + 14) % 16)
    to_sib = (dp, o, t)
    same = c == yl

    barrier = pltpu.get_barrier_semaphore()
    partners = (to_xr, to_xl, to_yp, to_zr, to_zl, to_sib, (dp, 0, ty), (dp, 1, ty))
    for who in partners:
        pl.semaphore_signal(barrier, inc=1, device_id=who, device_id_type=MESH)

    started = []
    arriving = {}
    tasks = {}

    def push(name, src, dst, who):
        i = len(started)
        copy = pltpu.make_async_remote_copy(
            src_ref=src, dst_ref=dst, send_sem=send.at[i], recv_sem=recv.at[i],
            device_id=who, device_id_type=MESH,
        )
        copy.start()
        started.append(copy)
        arriving.setdefault(name, []).append(copy)

    def wait(*names):
        for name in names:
            for copy in arriving.pop(name, ()):
                copy.wait_recv()

    locals_ = []

    def fetch(src, dst):
        copy = pltpu.make_async_copy(src, dst, local.at[len(locals_)])
        copy.start()
        locals_.append(copy)

    def col(i, n):
        return pl.ds(pl.multiple_of(i * n, n), n)

    def flip(k):
        return k + 1 - 2 * (k % 2)

    mine = pl.ds(pl.multiple_of(c * TOK, TOK), TOK)
    head = col(c, HEAD)
    head_o = col(o, HEAD)
    head_v = pl.ds(pl.multiple_of(256 + c * HEAD, HEAD), HEAD)
    head_vo = pl.ds(pl.multiple_of(256 + o * HEAD, HEAD), HEAD)

    def kv_rows(k, r0, n):
        return pl.ds(pl.multiple_of((2 * k + c) * 224 + r0, 16), n)

    def rows_of(buf):
        return lambda k, r0, n: buf.at[k, pl.ds(r0, n)]

    def slot_kv(k, r0, n):
        return wkv.at[kv_rows(k, r0, n)]

    def y_first(name, slot, r0, n):
        h = n // 2
        mine_ = slot(dp, r0, n)

        def from_y():
            wait(name + "y")
            s = slot(yp, r0, n)
            push(name + "fr", s, s, to_xr)
            push(name + "fl", s, s, to_xl)

        def near(first, second, a, b):
            def run():
                wait(name + first + "r", name + first + "l")
                lo, hi = slot(a, r0, h), slot(b, r0 + h, h)
                push(name + second + "0", lo, lo, to_xr)
                push(name + second + "1", hi, hi, to_xl)
            return run

        tasks[name + ".fy"] = from_y
        tasks[name + ".fx"] = near("", "h", xl, xr)
        tasks[name + ".fxf"] = near("f", "g", flip(xl), flip(xr))
        def start():
            push(name + "y", mine_, mine_, to_yp)
            push(name + "r", mine_, mine_, to_xr)
            push(name + "l", mine_, mine_, to_xl)

        starts[name] = start
        return [name + e for e in ("y", "r", "l", "fr", "fl", "h0", "h1", "g0", "g1")]

    def x_first(name, slot, r0, n):
        h = n // 2
        mine_ = slot(dp, r0, n)

        def from_x():
            wait(name + "r", name + "l")
            lo, hi = slot(xl, r0, h), slot(xr, r0 + h, h)
            push(name + "h0", lo, lo, to_xr)
            push(name + "h1", hi, hi, to_xl)
            a, b = slot(xl, r0, n), slot(xr, r0, n)
            push(name + "y0", a, a, to_yp)
            push(name + "y1", b, b, to_yp)

        def from_far():
            for i in (0, 1):
                wait(name + "h%d" % i)
                s = slot(far, r0 + i * h, h)
                push(name + "g%d" % i, s, s, to_yp)

        tasks[name + ".fx"] = from_x
        tasks[name + ".fxf"] = from_far
        def start():
            push(name + "r", mine_, mine_, to_xr)
            push(name + "l", mine_, mine_, to_xl)
            push(name + "y", mine_, mine_, to_yp)

        starts[name] = start
        return [name + e for e in ("y", "r", "l", "h0", "h1", "y0", "y1", "g0", "g1")]

    own_kv = kv_rows(dp, 0, 224)
    fetch(cot_in.at[0], stage)
    fetch(w_key, wkv.at[own_kv, pl.ds(0, 256)])
    fetch(w_value, wkv.at[own_kv, pl.ds(256, 256)])
    fetch(w_query, wq.at[dp])
    fetch(w_out, wo.at[dp])
    early = len(locals_)
    fetch(lag_in, lag)
    locals_[0].wait()
    pl.semaphore_wait(barrier, len(partners))

    cot_dst = cot.at[z, mine]
    cot_far = pltpu.make_async_remote_copy(
        src_ref=stage, dst_ref=cot_dst, send_sem=near_send.at[0], recv_sem=near_recv.at[c],
        device_id=(dp, yl, ty), device_id_type=MESH)
    cot_sib = pltpu.make_async_remote_copy(
        src_ref=stage, dst_ref=cot_dst, send_sem=near_send.at[1], recv_sem=near_recv.at[c],
        device_id=to_sib, device_id_type=MESH)
    cot_own = pltpu.make_async_copy(stage, cot_dst, near_recv.at[c])
    cot_far.start()

    @pl.when(same)
    def _():
        cot_own.start()

    @pl.when(jnp.logical_not(same))
    def _():
        cot_sib.start()

    starts = {}
    kv_all = y_first("kv", slot_kv, 0, 224)
    q_all, o_all = [], []
    if Q_Y:
        q_all += x_first("qA", rows_of(wq), 0, Q_Y)
    if Q_Y < 512:
        q_all += y_first("qB", rows_of(wq), Q_Y, 512 - Q_Y)
    if O_Y:
        o_all += x_first("oA", rows_of(wo), 0, O_Y)
    if O_Y < 256:
        o_all += y_first("oB", rows_of(wo), O_Y, 256 - O_Y)
    for copy in locals_[1:4]:
        copy.wait()
    for name in FIRST:
        starts.pop(name)()

    def own_o():
        locals_[4].wait()
        for name in sorted(starts, reverse=O_LAST_Y):
            starts[name]()

    tasks["own_o"] = own_o

    push("sib", augment.at[0], sts.at[mine], to_sib)
    fetch(augment.at[0], sts.at[mine])
    for k in range(NS):
        push("sib", anchor.at[0, :, pl.ds(pl.multiple_of((2 * k + o) * 512, 512), 512)], anc.at[k, mine], to_sib)
        fetch(anchor.at[0, :, pl.ds(pl.multiple_of((2 * k + c) * 512, 512), 512)], anc.at[k, mine])

    zero = jnp.zeros((224, 512), BF)
    for k in range(NS):
        wkv[pl.ds(pl.multiple_of((2 * k + o) * 224, 224), 224), :] = zero

    lo_tok, hi_tok = pl.ds(0, TOK), pl.ds(TOK, TOK)

    def ring(step, part_):
        def run():
            a, b = (lo_tok, hi_tok) if part_ == "a" else (hi_tok, lo_tok)
            if step == 1 and part_ == "a":
                for h in (0, 1):
                    got = cot.at[z, pl.ds(h * TOK, TOK)]
                    pltpu.make_async_copy(got, got, near_recv.at[h]).wait()
            if step > 1:
                wait("Z%d%s" % (step - 1, part_))
            s, r = cot.at[(z + 9 - step) % NS, a], cot.at[(z + step - 1) % NS, b]
            push("Z%d%s" % (step, part_), s, s, to_zr)
            push("Z%d%s" % (step, part_), r, r, to_zl)
        return run

    z_all = []
    for step in range(1, 5):
        for part_ in ("a", "b") if step < 4 else ("a",):
            tasks["z%d%s" % (step, part_)] = ring(step, part_)
            z_all.append("Z%d%s" % (step, part_))

    def turn(i):
        def run():
            if i == 0:
                wait("sib")
                for copy in locals_[early:]:
                    copy.wait()
            anc_t[i] = anc[i].T
            if i < 7:
                sts_t[pl.ds(i * 512, 512), :] = sts[:, pl.ds(i * 512, 512)].T
        return run

    for i in range(NS):
        tasks["turn%d" % i] = turn(i)

    def states_y():
        k = 2 * (z // 2) + 1 - dp % 2
        src = sts_t.at[pl.ds(pl.multiple_of((2 * k + c) * 224 + (z % 2) * 112, 112), 112)]
        push("E0", src, sts_y.at[pl.ds(pl.multiple_of(z * 112, 112), 112)], to_yp)

    def states_ring(step):
        def run():
            wait("E%d" % (step - 1))
            s = sts_y.at[pl.ds(pl.multiple_of(((z + 9 - step) % NS) * 112, 112), 112)]
            push("E%d" % step, s, s, to_zr)
            if step < 4:
                s = sts_y.at[pl.ds(pl.multiple_of(((z + step - 1) % NS) * 112, 112), 112)]
                push("E%d" % step, s, s, to_zl)
        return run

    tasks["e0"] = states_y
    for step in range(1, 5):
        tasks["e%d" % step] = states_ring(step)

    def keys_values():
        wait(*kv_all)
        part_kv[...] = nn(sts[:, pl.ds(0, 512)], wkv[pl.ds(0, 512), :])

        def add_kv(j, _):
            part_kv[...] += nn(sts[:, col(j, 512)], wkv[col(j, 512), :])
            return _

        lax.fori_loop(1, 7, add_kv, 0)
        push("exk", part_kv.at[:, head_o], other_kv.at[0], to_sib)
        push("exk", part_kv.at[:, head_vo], other_kv.at[1], to_sib)

    def queries_near():
        wait("qAy", "qAr", "qAl", "qBy", "qBr", "qBl")
        part[0] = nn(anc[dp], wq[dp])
        for k in (yp, xl, xr):
            part[0] += nn(anc[k], wq[k])

    def queries():
        wait(*q_all)
        for k in (flip(xl), flip(xr), far, flip(far)):
            part[0] += nn(anc[k], wq[k])
        push("exq", part.at[0, :, head_o], other.at[0], to_sib)

    factor = HEAD ** (-0.5)
    block = 128

    def attend(r):
        def run():
            if r == 0:
                wait("exk")
                k_h[...] = (part_kv[:, head] + other_kv[0]).astype(BF)
                v_h[...] = (part_kv[:, head_v] + other_kv[1]).astype(BF)
                wait("exq")
                q_h[...] = (part[0, :, head] + other[0]).astype(BF)
            rows = pl.ds(r * block, block)
            scores = nt(q_h[rows, :], k_h[...]) * factor
            reach = lax.broadcasted_iota(jnp.int32, (block, LEN), 0) + (r * block + lag[0])
            allowed = lax.broadcasted_iota(jnp.int32, (block, LEN), 1) <= reach
            scores = jnp.where(allowed, scores, -jnp.inf)
            expo = jnp.exp(scores - jnp.max(scores, axis=1, keepdims=True))
            p = expo / jnp.sum(expo, axis=1, keepdims=True)
            probs[rows, :] = p
            a = p.astype(BF)
            att[rows, :] = a
            ctx[rows, head] = nn(a, v_h[...]).astype(BF)
            push("ectx%d" % r, ctx.at[rows, head], ctx.at[rows, head], to_sib)
        return run

    tasks["kv"] = keys_values
    tasks["q0"] = queries_near
    tasks["q"] = queries
    for r in range(LEN // block):
        tasks["attn%d" % r] = attend(r)

    def back_context():
        wait(*o_all)
        wait(*z_all)
        part[1] = nt(cot[0], wo[0])

        def add_b(k, _):
            part[1] += nt(cot[k], wo[k])
            return _

        lax.fori_loop(1, NS, add_b, 0)
        push("eb", part.at[1, :, head_o], other.at[1], to_sib)

    tasks["bc"] = back_context

    def backward(r):
        def run():
            if r == 0:
                wait("eb")
                b_h[...] = (part[1, :, head] + other[1]).astype(BF)
            rows = pl.ds(r * block, block)
            dprobs = nt(b_h[rows, :], v_h[...])
            delta = jnp.sum(b_h[rows, :].astype(F32) * ctx[rows, head].astype(F32), axis=1, keepdims=True)
            ds = (probs[rows, :] * (dprobs - delta) * factor).astype(BF)
            qb[rows, head] = nn(ds, k_h[...]).astype(BF)
            kt = tn(ds, q_h[rows, :])
            vt = tn(att[rows, :], b_h[rows, :])
            if r == 0:
                other_kv[0] = kt
                other_kv[1] = vt
            else:
                other_kv[0] += kt
                other_kv[1] += vt
            if r == LEN // block - 1:
                kvb[:, head] = other_kv[0].astype(BF)
                kvb[:, head_v] = other_kv[1].astype(BF)
                push("KX", kvb.at[:, head], kvb_y.at[:, head], to_yp)
                push("KX", kvb.at[:, head_v], kvb_y.at[:, head_v], to_yp)
                push("ekb", kvb.at[:, head], kvb.at[:, head], to_sib)
                push("ekb", kvb.at[:, head_v], kvb.at[:, head_v], to_sib)
                push("ekb", qb.at[:, head], qb.at[:, head], to_sib)
        return run

    for r in range(LEN // block):
        tasks["bwd%d" % r] = backward(r)

    def hand_over():
        wait("KX")
        push("KF", kvb_y.at[:, head], kvb_y.at[:, head], to_sib)
        push("KF", kvb_y.at[:, head_v], kvb_y.at[:, head_v], to_sib)

    tasks["kvf"] = hand_over

    def slot(off, j):
        k = (dp + 2 * off + NS) % NS
        return flip(k) if j else k

    def add(s, k, rows, got):
        s[k, rows] = (s[k, rows].astype(F32) + got.astype(F32)).astype(BF)

    def sum_x_first(name, ready, s, r0, n, ra, rc, ry, make, out):
        h = n // 2
        lo, hi = pl.ds(r0, h), pl.ds(r0 + h, h)
        full = pl.ds(r0, n)

        def first(j):
            def run():
                ready()
                k = slot(2, j)
                make(k, r0, n)
                push(name + "a%d" % j, s.at[k, lo], ra.at[0, j], to_xr)
                push(name + "a%d" % j, s.at[k, hi], ra.at[1, j], to_xl)
            return run

        def second(j):
            def run():
                k, m = slot(1, j), slot(-1, j)
                make(k, r0, n)
                push(name + "b%d" % j, s.at[k, hi], rc.at[0, j, pl.ds(h, h)], to_xr)
                make(m, r0, n)
                push(name + "b%d" % j, s.at[m, lo], rc.at[1, j, pl.ds(0, h)], to_xl)
            return run

        def own():
            make(slot(0, 1), r0, n)
            make(slot(0, 0), r0, n)

        def on(j):
            def run():
                wait(name + "a%d" % j)
                k, m = slot(1, j), slot(-1, j)
                add(s, k, lo, ra[0, j])
                push(name + "p%d" % j, s.at[k, lo], rc.at[0, j, pl.ds(0, h)], to_xr)
                add(s, m, hi, ra[1, j])
                push(name + "p%d" % j, s.at[m, hi], rc.at[1, j, pl.ds(h, h)], to_xl)
            return run

        def total(j):
            wait(name + "b%d" % j, name + "p%d" % j)
            return s[slot(0, j), full].astype(F32) + rc[0, j].astype(F32) + rc[1, j].astype(F32)

        def across():
            k = slot(0, 1)
            s[k, full] = total(1).astype(BF)
            push(name + "y", s.at[k, full], ry, to_yp)

        def finish():
            both = total(0)
            wait(name + "y")
            out(both + ry[...].astype(F32), r0, n)

        for j in (0, 1):
            tasks[name + ".a%d" % j] = first(j)
            tasks[name + ".b%d" % j] = second(j)
            tasks[name + ".p%d" % j] = on(j)
        tasks[name + ".m0"] = own
        tasks[name + ".y"] = across
        tasks[name + ".f"] = finish

    def sum_y_first(name, ready, s, r0, n, ra, rc, ry, make, out):
        h = n // 2
        lo, hi = pl.ds(r0, h), pl.ds(r0 + h, h)
        full = pl.ds(r0, n)
        offs = (2, 1, -1, 0)

        def first(i):
            def run():
                ready()
                k = slot(offs[i], 1)
                make(k, r0, n)
                push(name + "y%d" % i, s.at[k, full], ry.at[i], to_yp)
            return run

        def own():
            for off in offs:
                make(slot(off, 0), r0, n)

        def from_y():
            wait(name + "y0")
            k = slot(2, 0)
            add(s, k, full, ry[0])
            push(name + "a", s.at[k, lo], ra.at[0], to_xr)
            push(name + "a_", s.at[k, hi], ra.at[1], to_xl)

        def right():
            wait(name + "y1")
            k = slot(1, 0)
            add(s, k, full, ry[1])
            push(name + "b", s.at[k, hi], rc.at[0, pl.ds(h, h)], to_xr)

        def left():
            wait(name + "y2")
            m = slot(-1, 0)
            add(s, m, full, ry[2])
            push(name + "b", s.at[m, lo], rc.at[1, pl.ds(0, h)], to_xl)

        def on_right():
            wait(name + "a")
            k = slot(1, 0)
            add(s, k, lo, ra[0])
            push(name + "p", s.at[k, lo], rc.at[0, pl.ds(0, h)], to_xr)

        def on_left():
            wait(name + "a_")
            m = slot(-1, 0)
            add(s, m, hi, ra[1])
            push(name + "p", s.at[m, hi], rc.at[1, pl.ds(h, h)], to_xl)

        def finish():
            wait(name + "y3", name + "b", name + "p")
            k = slot(0, 0)
            out(s[k, full].astype(F32) + ry[3].astype(F32) + rc[0].astype(F32) + rc[1].astype(F32), r0, n)

        for i in range(4):
            tasks[name + ".y%d" % i] = first(i)
        tasks[name + ".m"] = own
        tasks[name + ".a"] = from_y
        tasks[name + ".b"] = right
        tasks[name + ".b_"] = left
        tasks[name + ".p"] = on_right
        tasks[name + ".p_"] = on_left
        tasks[name + ".f"] = finish

    def sum_x(name, ready, s, n, ra, rc, make, out):
        h = n // 2
        lo, hi = pl.ds(0, h), pl.ds(h, h)

        def first():
            ready()
            k = slot(2, 0)
            make(k, 0, n)
            push(name + "a", s.at[k, lo], ra.at[0], to_xr)
            push(name + "a", s.at[k, hi], ra.at[1], to_xl)

        def second():
            k, m = slot(1, 0), slot(-1, 0)
            make(k, 0, n)
            push(name + "b", s.at[k, hi], rc.at[0, hi], to_xr)
            make(m, 0, n)
            push(name + "b", s.at[m, lo], rc.at[1, lo], to_xl)

        def own():
            make(slot(0, 0), 0, n)

        def on():
            wait(name + "a")
            k, m = slot(1, 0), slot(-1, 0)
            add(s, k, lo, ra[0])
            push(name + "p", s.at[k, lo], rc.at[0, lo], to_xr)
            add(s, m, hi, ra[1])
            push(name + "p", s.at[m, hi], rc.at[1, hi], to_xl)

        def finish():
            wait(name + "b", name + "p")
            out(s[slot(0, 0)].astype(F32) + rc[0].astype(F32) + rc[1].astype(F32), 0, n)

        tasks[name + ".a"] = first
        tasks[name + ".b"] = second
        tasks[name + ".m"] = own
        tasks[name + ".p"] = on
        tasks[name + ".f"] = finish

    def make_out(k, r0, n):
        s_out[k, pl.ds(r0, n)] = tn(ctx[:, pl.ds(r0, n)], cot[k]).astype(BF)

    def put_out(total, r0, n):
        g_out[pl.ds(r0, n)] = total.astype(BF)

    def make_kv(k, r0, n):
        own_ = nn(sts_t[pl.ds(pl.multiple_of((2 * k + c) * 224, 224), 224), :], kvb[...])
        s_kv[k] = (own_ + nn(sts_y[pl.ds(pl.multiple_of((k // 2) * 224, 224), 224), :], kvb_y[...])).astype(BF)

    def put_kv(total, r0, n):
        g_key[...] = total[:, :256].astype(BF)
        g_value[...] = total[:, 256:].astype(BF)

    def make_q(k, r0, n):
        s_q[k, pl.ds(r0, n)] = nn(anc_t[k, pl.ds(r0, n), :], qb[...]).astype(BF)

    def put_q(total, r0, n):
        g_query[pl.ds(r0, n)] = total.astype(BF)

    ctx_all = ["ectx%d" % r for r in range(LEN // block)]

    def ctx_ready():
        wait(*z_all)
        wait(*ctx_all)

    def back_ready():
        wait("ekb")

    def both_ready():
        wait("ekb", "KF", "E1", "E2", "E3", "E4")

    ra_oa, ra_ob = ra_out
    rc_oa, rc_ob = rc_out
    ry_oa, ry_ob = ry_out
    ra_qa, ra_qb = ra_q
    rc_qa, rc_qb = rc_q
    ry_qa, ry_qb = ry_q
    if GO_Y:
        sum_y_first("goA", ctx_ready, s_out, 0, GO_Y, ra_oa, rc_oa, ry_oa, make_out, put_out)
    if GO_Y < 256:
        sum_x_first("goB", ctx_ready, s_out, GO_Y, 256 - GO_Y, ra_ob, rc_ob, ry_ob, make_out, put_out)
    sum_x("gkv", both_ready, s_kv, 224, ra_kv, rc_kv, make_kv, put_kv)
    if GQ_Y:
        sum_y_first("gqA", back_ready, s_q, 0, GQ_Y, ra_qa, rc_qa, ry_qa, make_q, put_q)
    if GQ_Y < 512:
        sum_x_first("gqB", back_ready, s_q, GQ_Y, 512 - GQ_Y, ra_qb, rc_qb, ry_qb, make_q, put_q)

    def ring_add(step, part_):
        def run():
            a, b = (lo_tok, hi_tok) if part_ == "a" else (hi_tok, lo_tok)
            k, m = (z + 5 - step) % NS, (z + 3 + step) % NS
            if step > 1 and (step, part_) != (2, "b"):
                wait("U%d%s" % (step - 1, part_))
                add(upd, k, a, rz[0, step - 2, a])
                add(upd, m, b, rz[1, step - 2, b])
            if (step, part_) == (4, "a"):
                for i, name in enumerate(("U4a", "U4c")):
                    first_, second_ = pl.ds(i * 96, 96), pl.ds(TOK + i * 96, 96)
                    push(name, upd.at[k, first_], rz.at[0, 3, first_], to_zr)
                    push(name, upd.at[m, second_], rz.at[1, 3, second_], to_zl)
            else:
                push("U%d%s" % (step, part_), upd.at[k, a], rz.at[0, step - 1, a], to_zr)
                push("U%d%s" % (step, part_), upd.at[m, b], rz.at[1, step - 1, b], to_zl)
        return run

    def make_upd(off):
        k = (z + off) % NS
        upd[k] = nn(ctx[...], wo[k]).astype(BF)

    def updates_far():
        wait(*ctx_all)
        wait(*o_all)
        for off in (4, 3, 5):
            make_upd(off)
        ring_add(1, "a")()
        ring_add(2, "b")()

    def updates():
        for off in (2, 6, 1, 7, 0):
            make_upd(off)

    tasks["upd"] = updates_far
    tasks["upd2"] = updates
    for step in (2, 3, 4):
        for part_ in ("a", "b"):
            if (step, part_) != (2, "b"):
                tasks["u%d%s" % (step, part_)] = ring_add(step, part_)

    def last_copies(i):
        rows = pl.ds(i * 96, 96)

        def half(h):
            return upd.at[z, pl.ds(pl.multiple_of(h * TOK + i * 96, 96), 96)]

        own_ = pltpu.make_async_copy(half(c), ru.at[0, rows], fin_recv.at[2 * i])
        sib_ = pltpu.make_async_remote_copy(
            src_ref=half(o), dst_ref=ru.at[0, rows], send_sem=near_send.at[2 + 3 * i], recv_sem=fin_recv.at[2 * i],
            device_id=to_sib, device_id_type=MESH)
        far_ = [
            pltpu.make_async_remote_copy(
                src_ref=half(h), dst_ref=ru.at[1, rows], send_sem=near_send.at[3 + 3 * i + h],
                recv_sem=fin_recv.at[2 * i + 1], device_id=(dp, h, ty), device_id_type=MESH)
            for h in (0, 1)
        ]
        return own_, sib_, far_

    last = [last_copies(i) for i in (0, 1)]

    def last_exchange(i):
        def run():
            if i == 0:
                wait("U4a", "U4b")
            else:
                wait("U4c")
            for h in (0, 1):
                rows = pl.ds(h * TOK + i * 96, 96)
                upd[z, rows] = (
                    upd[z, rows].astype(F32) + rz[0, 3, rows].astype(F32) + rz[1, 3, rows].astype(F32)
                ).astype(BF)
            own_, sib_, far_ = last[i]

            @pl.when(same)
            def _():
                own_.start()
                sib_.start()

            @pl.when(jnp.logical_not(same))
            def _():
                far_[0].start()
                far_[1].start()
        return run

    def last_sum():
        for i in (0, 1):
            rows = pl.ds(i * 96, 96)
            for j in (0, 1):
                pltpu.make_async_copy(ru.at[j, rows], ru.at[j, rows], fin_recv.at[2 * i + j]).wait()
        update[0] = (ru[0].astype(F32) + ru[1].astype(F32)).astype(BF)

    tasks["u5"] = last_exchange(0)
    tasks["u6"] = last_exchange(1)
    tasks["ufin"] = last_sum

    steps = list(tasks.values())
    assert sorted(ORDER) == list(range(len(steps)))
    for i in ORDER:
        steps[i]()
    assert not arriving

    for copy in started:
        copy.wait_send()
    cot_far.wait_send()

    @pl.when(jnp.logical_not(same))
    def _():
        cot_sib.wait_send()
        for _, _, far_ in last:
            far_[0].wait_send()
            far_[1].wait_send()

    @pl.when(same)
    def _():
        for _, sib_, _ in last:
            sib_.wait_send()


def hand_on(*refs):
    copies = [pltpu.make_async_copy(refs[i], refs[5 + i], refs[10].at[i]) for i in range(5)]
    for copy in copies:
        copy.start()
    for copy in copies:
        copy.wait()


def local(*args):
    vm = pltpu.VMEM
    shapes = [
        ((1, TOK, 512), BF), ((512, 256), BF), ((224, 256), BF), ((224, 256), BF), ((256, 512), BF),
    ]

    def landing(n, width, cut):
        a, b = max(cut, 32), max(n - cut, 32)
        ra = [vm((2, a // 2, width), BF), vm((2, 2, b // 2, width), BF)]
        rc = [vm((2, a, width), BF), vm((2, 2, b, width), BF)]
        ry = [vm((4, a, width), BF), vm((b, width), BF)]
        return [ra, rc, ry]

    scratch = [
        vm((NS, LEN, 512), BF), vm((NS, 512, LEN), BF), vm((LEN, 3584), BF), vm((3584, LEN), BF),
        vm((NS, LEN, 512), BF), vm((NS, 512, 256), BF), vm((3584, 512), BF), vm((NS, 256, 512), BF),
        vm((NS, 256, 512), BF), vm((NS, 224, 512), BF), vm((NS, 512, 256), BF),
        vm((NS, LEN, 512), BF), vm((2, 4, LEN, 512), BF), vm((2, TOK, 512), BF),
        *landing(256, 512, GO_Y),
        vm((2, 112, 512), BF), vm((2, 224, 512), BF), vm((896, LEN), BF), vm((LEN, 512), BF),
        *landing(512, 256, GQ_Y),
        vm((2, LEN, 256), F32), vm((LEN, 512), F32), vm((2, LEN, HEAD), F32), vm((2, LEN, HEAD), F32),
        vm((LEN, HEAD), BF), vm((LEN, HEAD), BF), vm((LEN, HEAD), BF), vm((LEN, HEAD), BF),
        vm((LEN, LEN), F32), vm((LEN, LEN), BF), vm((LEN, 256), BF), vm((LEN, 256), BF), vm((LEN, 512), BF),
        pltpu.SMEM((1,), jnp.int32), vm((TOK, 512), BF),
        pltpu.SemaphoreType.DMA((COPIES,)), pltpu.SemaphoreType.DMA((COPIES,)),
        pltpu.SemaphoreType.DMA((8,)), pltpu.SemaphoreType.DMA((2,)), pltpu.SemaphoreType.DMA((4,)),
        pltpu.SemaphoreType.DMA((16,)),
    ]
    any_ = pl.BlockSpec(memory_space=pl.ANY)
    vmem = pl.BlockSpec(memory_space=pltpu.VMEM)
    results = [jax.ShapeDtypeStruct(s, d) for s, d in shapes]
    outs = pl.pallas_call(
        kernel,
        out_shape=[pltpu.VMEM(s, d) for s, d in shapes],
        in_specs=[any_, any_, pl.BlockSpec(memory_space=pltpu.HBM)] + [any_] * 5,
        out_specs=[vmem] * 5,
        scratch_shapes=scratch,
        compiler_params=pltpu.CompilerParams(
            collective_id=0, has_side_effects=True, vmem_limit_bytes=56 * 2**20
        ),
        name="block",
    )(*args)
    outs = [pltpu.with_memory_space_constraint(out, pltpu.VMEM) for out in outs]
    return pl.pallas_call(
        hand_on,
        out_shape=results,
        in_specs=[vmem] * 5,
        out_specs=[any_] * 5,
        scratch_shapes=[pltpu.SemaphoreType.DMA((5,))],
        name="hand_on",
    )(*outs)


def solution(mesh):
    placed = (
        P("dp", "seq", None),
        P("dp", "seq", None),
        P("dp"),
        P(("dp", "seq"), "tensor"),
        P(("dp", "seq"), "tensor"),
        P(("dp", "seq"), "tensor"),
        P("tensor", ("dp", "seq")),
        P("dp", "seq", "tensor"),
    )
    return jax.shard_map(
        local,
        mesh=mesh,
        in_specs=placed,
        out_specs=(
            P("dp", "seq", "tensor"),
            P(("dp", "seq"), "tensor"),
            P(("dp", "seq"), "tensor"),
            P(("dp", "seq"), "tensor"),
            P("tensor", ("dp", "seq")),
        ),
        check_vma=False,
    )
```

```python
import jax
import jax.numpy as jnp
from jax import lax
from jax.experimental import pallas as pl
from jax.experimental.pallas import tpu as pltpu
from jax.sharding import PartitionSpec as P

MESH = pl.DeviceIdType.MESH
BF = jnp.bfloat16
F32 = jnp.float32
HEAD = 128
TOK = 192
LEN = 384
NS = 8
COPIES = 256

Q_Y, O_Y, GQ_Y, GO_Y = 288, 128, 256, 96

FIRST = ('kv', 'qB', 'qA')
O_LAST_Y = bool(0)

ORDER = (
    14, 15, 1, 21, 6, 22, 23, 24, 0, 25, 26, 3, 27, 16, 28, 5, 29, 35, 17, 2, 18, 13, 4, 30, 7, 19, 34, 20, 8,
    10, 31, 11, 36, 9, 37, 38, 12, 39, 32, 56, 59, 57, 60, 45, 90, 91, 40, 46, 47, 48, 33, 62, 49, 58, 50, 41,
    61, 42, 92, 43, 51, 52, 94, 53, 54, 70, 71, 72, 73, 63, 81, 84, 82, 85, 74, 87, 55, 44, 83, 93, 86, 65,
    66, 75, 67, 96, 76, 88, 77, 95, 68, 78, 79, 64, 97, 98, 89, 69, 80, 99,
)

SWEEPS = (96,)
EARLY = 130


def nn(a, b):
    return jnp.dot(a, b, preferred_element_type=F32)


def nt(a, b):
    return lax.dot_general(a, b, (((1,), (1,)), ((), ())), preferred_element_type=F32)


def tn(a, b):
    return lax.dot_general(a, b, (((0,), (0,)), ((), ())), preferred_element_type=F32)


def kernel(
    anchor, augment, lag_in, w_query, w_key, w_value, w_out, cot_in,
    update, g_query, g_key, g_value, g_out,
    anc, anc_t, sts, sts_t, cot, wq, wkv, wo,
    s_out, s_kv, s_q, upd, rz, ru,
    ra_out, rc_out, ry_out, ra_kv, rc_kv, sts_y, kvb_y, ra_q, rc_q, ry_q,
    part, part_kv, other, other_kv, q_h, k_h, v_h, b_h, probs, att, ctx, qb, kvb,
    lag, stage,
    send, recv, near_send, near_recv, fin_recv, local,
):
    dp, c, t = lax.axis_index("dp"), lax.axis_index("seq"), lax.axis_index("tensor")
    z, yl = t // 2, t % 2
    o = 1 - c
    xr, xl = (dp + 2) % NS, (dp + 6) % NS
    far = (dp + 4) % NS
    yp = dp + 1 - 2 * (dp % 2)
    ty = t + 1 - 2 * yl
    to_xr, to_xl, to_yp = (xr, c, t), (xl, c, t), (yp, c, t)
    to_zr, to_zl = (dp, c, (t + 2) % 16), (dp, c, (t + 14) % 16)
    to_sib = (dp, o, t)
    same = c == yl

    barrier = pltpu.get_barrier_semaphore()
    partners = (to_xr, to_xl, to_yp, to_zr, to_zl, to_sib, (dp, 0, ty), (dp, 1, ty))
    for who in partners:
        pl.semaphore_signal(barrier, inc=1, device_id=who, device_id_type=MESH)

    started = []
    arriving = {}
    tasks = {}

    def push(name, src, dst, who):
        i = len(started)
        copy = pltpu.make_async_remote_copy(
            src_ref=src, dst_ref=dst, send_sem=send.at[i], recv_sem=recv.at[i],
            device_id=who, device_id_type=MESH,
        )
        copy.start()
        started.append(copy)
        arriving.setdefault(name, []).append(copy)

    def wait(*names):
        for name in names:
            for copy in arriving.pop(name, ()):
                copy.wait_recv()

    locals_ = []

    def fetch(src, dst):
        copy = pltpu.make_async_copy(src, dst, local.at[len(locals_)])
        copy.start()
        locals_.append(copy)

    def col(i, n):
        return pl.ds(pl.multiple_of(i * n, n), n)

    def flip(k):
        return k + 1 - 2 * (k % 2)

    mine = pl.ds(pl.multiple_of(c * TOK, TOK), TOK)
    head = col(c, HEAD)
    head_o = col(o, HEAD)
    head_v = pl.ds(pl.multiple_of(256 + c * HEAD, HEAD), HEAD)
    head_vo = pl.ds(pl.multiple_of(256 + o * HEAD, HEAD), HEAD)

    def kv_rows(k, r0, n):
        return pl.ds(pl.multiple_of((2 * k + c) * 224 + r0, 16), n)

    def rows_of(buf):
        return lambda k, r0, n: buf.at[k, pl.ds(r0, n)]

    def slot_kv(k, r0, n):
        return wkv.at[kv_rows(k, r0, n)]

    def y_first(name, slot, r0, n):
        h = n // 2
        mine_ = slot(dp, r0, n)

        def from_y():
            wait(name + "y")
            s = slot(yp, r0, n)
            push(name + "fr", s, s, to_xr)
            push(name + "fl", s, s, to_xl)

        def near(first, second, a, b):
            def run():
                wait(name + first + "r", name + first + "l")
                lo, hi = slot(a, r0, h), slot(b, r0 + h, h)
                push(name + second + "0", lo, lo, to_xr)
                push(name + second + "1", hi, hi, to_xl)
            return run

        tasks[name + ".fy"] = from_y
        tasks[name + ".fx"] = near("", "h", xl, xr)
        tasks[name + ".fxf"] = near("f", "g", flip(xl), flip(xr))
        def start():
            push(name + "y", mine_, mine_, to_yp)
            push(name + "r", mine_, mine_, to_xr)
            push(name + "l", mine_, mine_, to_xl)

        starts[name] = start
        return [name + e for e in ("y", "r", "l", "fr", "fl", "h0", "h1", "g0", "g1")]

    def x_first(name, slot, r0, n):
        h = n // 2
        mine_ = slot(dp, r0, n)

        def from_x():
            wait(name + "r", name + "l")
            lo, hi = slot(xl, r0, h), slot(xr, r0 + h, h)
            push(name + "h0", lo, lo, to_xr)
            push(name + "h1", hi, hi, to_xl)
            a, b = slot(xl, r0, n), slot(xr, r0, n)
            push(name + "y0", a, a, to_yp)
            push(name + "y1", b, b, to_yp)

        def from_far():
            for i in (0, 1):
                wait(name + "h%d" % i)
                s = slot(far, r0 + i * h, h)
                push(name + "g%d" % i, s, s, to_yp)

        tasks[name + ".fx"] = from_x
        tasks[name + ".fxf"] = from_far
        def start():
            push(name + "r", mine_, mine_, to_xr)
            push(name + "l", mine_, mine_, to_xl)
            push(name + "y", mine_, mine_, to_yp)

        starts[name] = start
        return [name + e for e in ("y", "r", "l", "h0", "h1", "y0", "y1", "g0", "g1")]

    own_kv = kv_rows(dp, 0, 224)
    fetch(cot_in.at[0], stage)
    fetch(w_key, wkv.at[own_kv, pl.ds(0, 256)])
    fetch(w_value, wkv.at[own_kv, pl.ds(256, 256)])
    fetch(w_query, wq.at[dp])
    fetch(w_out, wo.at[dp])
    early = len(locals_)
    fetch(lag_in, lag)
    locals_[0].wait()
    pl.semaphore_wait(barrier, len(partners))

    cot_dst = cot.at[z, mine]
    cot_far = pltpu.make_async_remote_copy(
        src_ref=stage, dst_ref=cot_dst, send_sem=near_send.at[0], recv_sem=near_recv.at[c],
        device_id=(dp, yl, ty), device_id_type=MESH)
    cot_sib = pltpu.make_async_remote_copy(
        src_ref=stage, dst_ref=cot_dst, send_sem=near_send.at[1], recv_sem=near_recv.at[c],
        device_id=to_sib, device_id_type=MESH)
    cot_own = pltpu.make_async_copy(stage, cot_dst, near_recv.at[c])
    cot_far.start()

    @pl.when(same)
    def _():
        cot_own.start()

    @pl.when(jnp.logical_not(same))
    def _():
        cot_sib.start()

    starts = {}
    kv_all = y_first("kv", slot_kv, 0, 224)
    q_all, o_all = [], []
    if Q_Y:
        q_all += x_first("qA", rows_of(wq), 0, Q_Y)
    if Q_Y < 512:
        q_all += y_first("qB", rows_of(wq), Q_Y, 512 - Q_Y)
    if O_Y:
        o_all += x_first("oA", rows_of(wo), 0, O_Y)
    if O_Y < 256:
        o_all += y_first("oB", rows_of(wo), O_Y, 256 - O_Y)
    for copy in locals_[1:4]:
        copy.wait()
    for name in FIRST:
        starts.pop(name)()

    def own_o():
        locals_[4].wait()
        for name in sorted(starts, reverse=O_LAST_Y):
            starts[name]()

    tasks["own_o"] = own_o

    push("sib", augment.at[0], sts.at[mine], to_sib)
    fetch(augment.at[0], sts.at[mine])
    for k in range(NS):
        push("sib", anchor.at[0, :, pl.ds(pl.multiple_of((2 * k + o) * 512, 512), 512)], anc.at[k, mine], to_sib)
        fetch(anchor.at[0, :, pl.ds(pl.multiple_of((2 * k + c) * 512, 512), 512)], anc.at[k, mine])

    zero = jnp.zeros((224, 512), BF)
    for k in range(NS):
        wkv[pl.ds(pl.multiple_of((2 * k + o) * 224, 224), 224), :] = zero

    lo_tok, hi_tok = pl.ds(0, TOK), pl.ds(TOK, TOK)

    def ring(step, part_):
        def run():
            a, b = (lo_tok, hi_tok) if part_ == "a" else (hi_tok, lo_tok)
            if step == 1 and part_ == "a":
                for h in (0, 1):
                    got = cot.at[z, pl.ds(h * TOK, TOK)]
                    pltpu.make_async_copy(got, got, near_recv.at[h]).wait()
            if step > 1:
                wait("Z%d%s" % (step - 1, part_))
            s, r = cot.at[(z + 9 - step) % NS, a], cot.at[(z + step - 1) % NS, b]
            push("Z%d%s" % (step, part_), s, s, to_zr)
            push("Z%d%s" % (step, part_), r, r, to_zl)
        return run

    z_all = []
    for step in range(1, 5):
        for part_ in ("a", "b") if step < 4 else ("a",):
            tasks["z%d%s" % (step, part_)] = ring(step, part_)
            z_all.append("Z%d%s" % (step, part_))

    def turn(i):
        def run():
            if i == 0:
                wait("sib")
                for copy in locals_[early:]:
                    copy.wait()
            anc_t[i] = anc[i].T
            if i < 7:
                sts_t[pl.ds(i * 512, 512), :] = sts[:, pl.ds(i * 512, 512)].T
        return run

    for i in range(NS):
        tasks["turn%d" % i] = turn(i)

    def states_y():
        k = 2 * (z // 2) + 1 - dp % 2
        src = sts_t.at[pl.ds(pl.multiple_of((2 * k + c) * 224 + (z % 2) * 112, 112), 112)]
        push("E0", src, sts_y.at[pl.ds(pl.multiple_of(z * 112, 112), 112)], to_yp)

    def states_ring(step):
        def run():
            wait("E%d" % (step - 1))
            s = sts_y.at[pl.ds(pl.multiple_of(((z + 9 - step) % NS) * 112, 112), 112)]
            push("E%d" % step, s, s, to_zr)
            if step < 4:
                s = sts_y.at[pl.ds(pl.multiple_of(((z + step - 1) % NS) * 112, 112), 112)]
                push("E%d" % step, s, s, to_zl)
        return run

    tasks["e0"] = states_y
    for step in range(1, 5):
        tasks["e%d" % step] = states_ring(step)

    def keys_values():
        wait(*kv_all)
        part_kv[...] = nn(sts[:, pl.ds(0, 512)], wkv[pl.ds(0, 512), :])

        def add_kv(j, _):
            part_kv[...] += nn(sts[:, col(j, 512)], wkv[col(j, 512), :])
            return _

        lax.fori_loop(1, 7, add_kv, 0)
        push("exk", part_kv.at[:, head_o], other_kv.at[0], to_sib)
        push("exk", part_kv.at[:, head_vo], other_kv.at[1], to_sib)

    def queries_near():
        wait("qAy", "qAr", "qAl", "qBy", "qBr", "qBl")
        part[0] = nn(anc[dp], wq[dp])
        for k in (yp, xl, xr):
            part[0] += nn(anc[k], wq[k])

    def queries():
        wait(*q_all)
        for k in (flip(xl), flip(xr), far, flip(far)):
            part[0] += nn(anc[k], wq[k])
        push("exq", part.at[0, :, head_o], other.at[0], to_sib)

    factor = HEAD ** (-0.5)
    block = 128

    def attend(r):
        def run():
            if r == 0:
                wait("exk")
                k_h[...] = (part_kv[:, head] + other_kv[0]).astype(BF)
                v_h[...] = (part_kv[:, head_v] + other_kv[1]).astype(BF)
                wait("exq")
                q_h[...] = (part[0, :, head] + other[0]).astype(BF)
            rows = pl.ds(r * block, block)
            scores = nt(q_h[rows, :], k_h[...]) * factor
            reach = lax.broadcasted_iota(jnp.int32, (block, LEN), 0) + (r * block + lag[0])
            allowed = lax.broadcasted_iota(jnp.int32, (block, LEN), 1) <= reach
            scores = jnp.where(allowed, scores, -jnp.inf)
            expo = jnp.exp(scores - jnp.max(scores, axis=1, keepdims=True))
            p = expo / jnp.sum(expo, axis=1, keepdims=True)
            probs[rows, :] = p
            a = p.astype(BF)
            att[rows, :] = a
            ctx[rows, head] = nn(a, v_h[...]).astype(BF)
            push("ectx%d" % r, ctx.at[rows, head], ctx.at[rows, head], to_sib)
        return run

    tasks["kv"] = keys_values
    tasks["q0"] = queries_near
    tasks["q"] = queries
    for r in range(LEN // block):
        tasks["attn%d" % r] = attend(r)

    def back_context():
        wait(*o_all)
        wait(*z_all)
        part[1] = nt(cot[0], wo[0])

        def add_b(k, _):
            part[1] += nt(cot[k], wo[k])
            return _

        lax.fori_loop(1, NS, add_b, 0)
        push("eb", part.at[1, :, head_o], other.at[1], to_sib)

    tasks["bc"] = back_context

    def backward(r):
        def run():
            if r == 0:
                wait("eb")
                b_h[...] = (part[1, :, head] + other[1]).astype(BF)
            rows = pl.ds(r * block, block)
            dprobs = nt(b_h[rows, :], v_h[...])
            delta = jnp.sum(b_h[rows, :].astype(F32) * ctx[rows, head].astype(F32), axis=1, keepdims=True)
            ds = (probs[rows, :] * (dprobs - delta) * factor).astype(BF)
            qb[rows, head] = nn(ds, k_h[...]).astype(BF)
            kt = tn(ds, q_h[rows, :])
            vt = tn(att[rows, :], b_h[rows, :])
            if r == 0:
                other_kv[0] = kt
                other_kv[1] = vt
            else:
                other_kv[0] += kt
                other_kv[1] += vt
            if r == LEN // block - 1:
                kvb[:, head] = other_kv[0].astype(BF)
                kvb[:, head_v] = other_kv[1].astype(BF)
                push("KX", kvb.at[:, head], kvb_y.at[:, head], to_yp)
                push("KX", kvb.at[:, head_v], kvb_y.at[:, head_v], to_yp)
                push("ekb", kvb.at[:, head], kvb.at[:, head], to_sib)
                push("ekb", kvb.at[:, head_v], kvb.at[:, head_v], to_sib)
                push("ekb", qb.at[:, head], qb.at[:, head], to_sib)
        return run

    for r in range(LEN // block):
        tasks["bwd%d" % r] = backward(r)

    def hand_over():
        wait("KX")
        push("KF", kvb_y.at[:, head], kvb_y.at[:, head], to_sib)
        push("KF", kvb_y.at[:, head_v], kvb_y.at[:, head_v], to_sib)

    tasks["kvf"] = hand_over

    def slot(off, j):
        k = (dp + 2 * off + NS) % NS
        return flip(k) if j else k

    def add(s, k, rows, got):
        s[k, rows] = (s[k, rows].astype(F32) + got.astype(F32)).astype(BF)

    def sum_x_first(name, ready, s, r0, n, ra, rc, ry, make, out):
        h = n // 2
        lo, hi = pl.ds(r0, h), pl.ds(r0 + h, h)
        full = pl.ds(r0, n)

        def first(j):
            def run():
                ready()
                k = slot(2, j)
                make(k, r0, n)
                push(name + "a%d" % j, s.at[k, lo], ra.at[0, j], to_xr)
                push(name + "a%d" % j, s.at[k, hi], ra.at[1, j], to_xl)
            return run

        def second(j):
            def run():
                k, m = slot(1, j), slot(-1, j)
                make(k, r0, n)
                push(name + "b%d" % j, s.at[k, hi], rc.at[0, j, pl.ds(h, h)], to_xr)
                make(m, r0, n)
                push(name + "b%d" % j, s.at[m, lo], rc.at[1, j, pl.ds(0, h)], to_xl)
            return run

        def own():
            make(slot(0, 1), r0, n)
            make(slot(0, 0), r0, n)

        def on(j):
            def run():
                wait(name + "a%d" % j)
                k, m = slot(1, j), slot(-1, j)
                add(s, k, lo, ra[0, j])
                push(name + "p%d" % j, s.at[k, lo], rc.at[0, j, pl.ds(0, h)], to_xr)
                add(s, m, hi, ra[1, j])
                push(name + "p%d" % j, s.at[m, hi], rc.at[1, j, pl.ds(h, h)], to_xl)
            return run

        def total(j):
            wait(name + "b%d" % j, name + "p%d" % j)
            return s[slot(0, j), full].astype(F32) + rc[0, j].astype(F32) + rc[1, j].astype(F32)

        def across():
            k = slot(0, 1)
            s[k, full] = total(1).astype(BF)
            push(name + "y", s.at[k, full], ry, to_yp)

        def finish():
            both = total(0)
            wait(name + "y")
            out(both + ry[...].astype(F32), r0, n)

        for j in (0, 1):
            tasks[name + ".a%d" % j] = first(j)
            tasks[name + ".b%d" % j] = second(j)
            tasks[name + ".p%d" % j] = on(j)
        tasks[name + ".m0"] = own
        tasks[name + ".y"] = across
        tasks[name + ".f"] = finish

    def sum_y_first(name, ready, s, r0, n, ra, rc, ry, make, out):
        h = n // 2
        lo, hi = pl.ds(r0, h), pl.ds(r0 + h, h)
        full = pl.ds(r0, n)
        offs = (2, 1, -1, 0)

        def first(i):
            def run():
                ready()
                k = slot(offs[i], 1)
                make(k, r0, n)
                push(name + "y%d" % i, s.at[k, full], ry.at[i], to_yp)
            return run

        def own():
            for off in offs:
                make(slot(off, 0), r0, n)

        def from_y():
            wait(name + "y0")
            k = slot(2, 0)
            add(s, k, full, ry[0])
            push(name + "a", s.at[k, lo], ra.at[0], to_xr)
            push(name + "a_", s.at[k, hi], ra.at[1], to_xl)

        def right():
            wait(name + "y1")
            k = slot(1, 0)
            add(s, k, full, ry[1])
            push(name + "b", s.at[k, hi], rc.at[0, pl.ds(h, h)], to_xr)

        def left():
            wait(name + "y2")
            m = slot(-1, 0)
            add(s, m, full, ry[2])
            push(name + "b", s.at[m, lo], rc.at[1, pl.ds(0, h)], to_xl)

        def on_right():
            wait(name + "a")
            k = slot(1, 0)
            add(s, k, lo, ra[0])
            push(name + "p", s.at[k, lo], rc.at[0, pl.ds(0, h)], to_xr)

        def on_left():
            wait(name + "a_")
            m = slot(-1, 0)
            add(s, m, hi, ra[1])
            push(name + "p", s.at[m, hi], rc.at[1, pl.ds(h, h)], to_xl)

        def finish():
            wait(name + "y3", name + "b", name + "p")
            k = slot(0, 0)
            out(s[k, full].astype(F32) + ry[3].astype(F32) + rc[0].astype(F32) + rc[1].astype(F32), r0, n)

        for i in range(4):
            tasks[name + ".y%d" % i] = first(i)
        tasks[name + ".m"] = own
        tasks[name + ".a"] = from_y
        tasks[name + ".b"] = right
        tasks[name + ".b_"] = left
        tasks[name + ".p"] = on_right
        tasks[name + ".p_"] = on_left
        tasks[name + ".f"] = finish

    def sum_x(name, ready, s, n, ra, rc, make, out):
        h = n // 2
        lo, hi = pl.ds(0, h), pl.ds(h, h)

        def first():
            ready()
            k = slot(2, 0)
            make(k, 0, n)
            push(name + "a", s.at[k, lo], ra.at[0], to_xr)
            push(name + "a", s.at[k, hi], ra.at[1], to_xl)

        def second():
            k, m = slot(1, 0), slot(-1, 0)
            make(k, 0, n)
            push(name + "b", s.at[k, hi], rc.at[0, hi], to_xr)
            make(m, 0, n)
            push(name + "b", s.at[m, lo], rc.at[1, lo], to_xl)

        def own():
            make(slot(0, 0), 0, n)

        def on():
            wait(name + "a")
            k, m = slot(1, 0), slot(-1, 0)
            add(s, k, lo, ra[0])
            push(name + "p", s.at[k, lo], rc.at[0, lo], to_xr)
            add(s, m, hi, ra[1])
            push(name + "p", s.at[m, hi], rc.at[1, hi], to_xl)

        def finish():
            wait(name + "b", name + "p")
            out(s[slot(0, 0)].astype(F32) + rc[0].astype(F32) + rc[1].astype(F32), 0, n)

        tasks[name + ".a"] = first
        tasks[name + ".b"] = second
        tasks[name + ".m"] = own
        tasks[name + ".p"] = on
        tasks[name + ".f"] = finish

    def make_out(k, r0, n):
        s_out[k, pl.ds(r0, n)] = tn(ctx[:, pl.ds(r0, n)], cot[k]).astype(BF)

    def put_out(total, r0, n):
        g_out[pl.ds(r0, n)] = total.astype(BF)

    def make_kv(k, r0, n):
        own_ = nn(sts_t[pl.ds(pl.multiple_of((2 * k + c) * 224, 224), 224), :], kvb[...])
        s_kv[k] = (own_ + nn(sts_y[pl.ds(pl.multiple_of((k // 2) * 224, 224), 224), :], kvb_y[...])).astype(BF)

    def put_kv(total, r0, n):
        g_key[...] = total[:, :256].astype(BF)
        g_value[...] = total[:, 256:].astype(BF)

    def make_q(k, r0, n):
        s_q[k, pl.ds(r0, n)] = nn(anc_t[k, pl.ds(r0, n), :], qb[...]).astype(BF)

    def put_q(total, r0, n):
        g_query[pl.ds(r0, n)] = total.astype(BF)

    ctx_all = ["ectx%d" % r for r in range(LEN // block)]

    def ctx_ready():
        wait(*z_all)
        wait(*ctx_all)

    def back_ready():
        wait("ekb")

    def both_ready():
        wait("ekb", "KF", "E1", "E2", "E3", "E4")

    ra_oa, ra_ob = ra_out
    rc_oa, rc_ob = rc_out
    ry_oa, ry_ob = ry_out
    ra_qa, ra_qb = ra_q
    rc_qa, rc_qb = rc_q
    ry_qa, ry_qb = ry_q
    if GO_Y:
        sum_y_first("goA", ctx_ready, s_out, 0, GO_Y, ra_oa, rc_oa, ry_oa, make_out, put_out)
    if GO_Y < 256:
        sum_x_first("goB", ctx_ready, s_out, GO_Y, 256 - GO_Y, ra_ob, rc_ob, ry_ob, make_out, put_out)
    sum_x("gkv", both_ready, s_kv, 224, ra_kv, rc_kv, make_kv, put_kv)
    if GQ_Y:
        sum_y_first("gqA", back_ready, s_q, 0, GQ_Y, ra_qa, rc_qa, ry_qa, make_q, put_q)
    if GQ_Y < 512:
        sum_x_first("gqB", back_ready, s_q, GQ_Y, 512 - GQ_Y, ra_qb, rc_qb, ry_qb, make_q, put_q)

    def ring_add(step, part_):
        def run():
            a, b = (lo_tok, hi_tok) if part_ == "a" else (hi_tok, lo_tok)
            k, m = (z + 5 - step) % NS, (z + 3 + step) % NS
            if step > 1 and (step, part_) != (2, "b"):
                wait("U%d%s" % (step - 1, part_))
                add(upd, k, a, rz[0, step - 2, a])
                add(upd, m, b, rz[1, step - 2, b])
            if (step, part_) == (4, "a"):
                for i, name in enumerate(("U4a", "U4c")):
                    first_, second_ = pl.ds(i * 96, 96), pl.ds(TOK + i * 96, 96)
                    push(name, upd.at[k, first_], rz.at[0, 3, first_], to_zr)
                    push(name, upd.at[m, second_], rz.at[1, 3, second_], to_zl)
            else:
                push("U%d%s" % (step, part_), upd.at[k, a], rz.at[0, step - 1, a], to_zr)
                push("U%d%s" % (step, part_), upd.at[m, b], rz.at[1, step - 1, b], to_zl)
        return run

    def make_upd(off):
        k = (z + off) % NS
        upd[k] = nn(ctx[...], wo[k]).astype(BF)

    def updates_far():
        wait(*ctx_all)
        wait(*o_all)
        for off in (4, 3, 5):
            make_upd(off)
        ring_add(1, "a")()
        ring_add(2, "b")()

    def updates():
        for off in (2, 6, 1, 7, 0):
            make_upd(off)

    tasks["upd"] = updates_far
    tasks["upd2"] = updates
    for step in (2, 3, 4):
        for part_ in ("a", "b"):
            if (step, part_) != (2, "b"):
                tasks["u%d%s" % (step, part_)] = ring_add(step, part_)

    def last_copies(i):
        rows = pl.ds(i * 96, 96)

        def half(h):
            return upd.at[z, pl.ds(pl.multiple_of(h * TOK + i * 96, 96), 96)]

        own_ = pltpu.make_async_copy(half(c), ru.at[0, rows], fin_recv.at[2 * i])
        sib_ = pltpu.make_async_remote_copy(
            src_ref=half(o), dst_ref=ru.at[0, rows], send_sem=near_send.at[2 + 3 * i], recv_sem=fin_recv.at[2 * i],
            device_id=to_sib, device_id_type=MESH)
        far_ = [
            pltpu.make_async_remote_copy(
                src_ref=half(h), dst_ref=ru.at[1, rows], send_sem=near_send.at[3 + 3 * i + h],
                recv_sem=fin_recv.at[2 * i + 1], device_id=(dp, h, ty), device_id_type=MESH)
            for h in (0, 1)
        ]
        return own_, sib_, far_

    last = [last_copies(i) for i in (0, 1)]

    def last_exchange(i):
        def run():
            if i == 0:
                wait("U4a", "U4b")
            else:
                wait("U4c")
            for h in (0, 1):
                rows = pl.ds(h * TOK + i * 96, 96)
                upd[z, rows] = (
                    upd[z, rows].astype(F32) + rz[0, 3, rows].astype(F32) + rz[1, 3, rows].astype(F32)
                ).astype(BF)
            own_, sib_, far_ = last[i]

            @pl.when(same)
            def _():
                own_.start()
                sib_.start()

            @pl.when(jnp.logical_not(same))
            def _():
                far_[0].start()
                far_[1].start()
        return run

    def last_sum():
        for i in (0, 1):
            rows = pl.ds(i * 96, 96)
            for j in (0, 1):
                pltpu.make_async_copy(ru.at[j, rows], ru.at[j, rows], fin_recv.at[2 * i + j]).wait()
        update[0] = (ru[0].astype(F32) + ru[1].astype(F32)).astype(BF)

    tasks["u5"] = last_exchange(0)
    tasks["u6"] = last_exchange(1)
    tasks["ufin"] = last_sum

    steps = list(tasks.values())
    assert sorted(ORDER) == list(range(len(steps)))
    gone = 0
    for n, i in enumerate(ORDER):
        if n in SWEEPS:
            for copy in started[:EARLY]:
                copy.wait_send()
            gone = EARLY
        steps[i]()
    assert not arriving

    for copy in started[gone:]:
        copy.wait_send()
    cot_far.wait_send()

    @pl.when(jnp.logical_not(same))
    def _():
        cot_sib.wait_send()
        for _, _, far_ in last:
            far_[0].wait_send()
            far_[1].wait_send()

    @pl.when(same)
    def _():
        for _, sib_, _ in last:
            sib_.wait_send()


def hand_on(*refs):
    copies = [pltpu.make_async_copy(refs[i], refs[5 + i], refs[10].at[i]) for i in range(5)]
    for copy in copies:
        copy.start()
    for copy in copies:
        copy.wait()


def local(*args):
    vm = pltpu.VMEM
    shapes = [
        ((1, TOK, 512), BF), ((512, 256), BF), ((224, 256), BF), ((224, 256), BF), ((256, 512), BF),
    ]

    def landing(n, width, cut):
        a, b = max(cut, 32), max(n - cut, 32)
        ra = [vm((2, a // 2, width), BF), vm((2, 2, b // 2, width), BF)]
        rc = [vm((2, a, width), BF), vm((2, 2, b, width), BF)]
        ry = [vm((4, a, width), BF), vm((b, width), BF)]
        return [ra, rc, ry]

    scratch = [
        vm((NS, LEN, 512), BF), vm((NS, 512, LEN), BF), vm((LEN, 3584), BF), vm((3584, LEN), BF),
        vm((NS, LEN, 512), BF), vm((NS, 512, 256), BF), vm((3584, 512), BF), vm((NS, 256, 512), BF),
        vm((NS, 256, 512), BF), vm((NS, 224, 512), BF), vm((NS, 512, 256), BF),
        vm((NS, LEN, 512), BF), vm((2, 4, LEN, 512), BF), vm((2, TOK, 512), BF),
        *landing(256, 512, GO_Y),
        vm((2, 112, 512), BF), vm((2, 224, 512), BF), vm((896, LEN), BF), vm((LEN, 512), BF),
        *landing(512, 256, GQ_Y),
        vm((2, LEN, 256), F32), vm((LEN, 512), F32), vm((2, LEN, HEAD), F32), vm((2, LEN, HEAD), F32),
        vm((LEN, HEAD), BF), vm((LEN, HEAD), BF), vm((LEN, HEAD), BF), vm((LEN, HEAD), BF),
        vm((LEN, LEN), F32), vm((LEN, LEN), BF), vm((LEN, 256), BF), vm((LEN, 256), BF), vm((LEN, 512), BF),
        pltpu.SMEM((1,), jnp.int32), vm((TOK, 512), BF),
        pltpu.SemaphoreType.DMA((COPIES,)), pltpu.SemaphoreType.DMA((COPIES,)),
        pltpu.SemaphoreType.DMA((8,)), pltpu.SemaphoreType.DMA((2,)), pltpu.SemaphoreType.DMA((4,)),
        pltpu.SemaphoreType.DMA((16,)),
    ]
    any_ = pl.BlockSpec(memory_space=pl.ANY)
    vmem = pl.BlockSpec(memory_space=pltpu.VMEM)
    results = [jax.ShapeDtypeStruct(s, d) for s, d in shapes]
    outs = pl.pallas_call(
        kernel,
        out_shape=[pltpu.VMEM(s, d) for s, d in shapes],
        in_specs=[any_, any_, pl.BlockSpec(memory_space=pltpu.HBM)] + [any_] * 5,
        out_specs=[vmem] * 5,
        scratch_shapes=scratch,
        compiler_params=pltpu.CompilerParams(
            collective_id=0, has_side_effects=True, vmem_limit_bytes=56 * 2**20
        ),
        name="block",
    )(*args)
    outs = [pltpu.with_memory_space_constraint(out, pltpu.VMEM) for out in outs]
    return pl.pallas_call(
        hand_on,
        out_shape=results,
        in_specs=[vmem] * 5,
        out_specs=[any_] * 5,
        scratch_shapes=[pltpu.SemaphoreType.DMA((5,))],
        name="hand_on",
    )(*outs)


def solution(mesh):
    placed = (
        P("dp", "seq", None),
        P("dp", "seq", None),
        P("dp"),
        P(("dp", "seq"), "tensor"),
        P(("dp", "seq"), "tensor"),
        P(("dp", "seq"), "tensor"),
        P("tensor", ("dp", "seq")),
        P("dp", "seq", "tensor"),
    )
    return jax.shard_map(
        local,
        mesh=mesh,
        in_specs=placed,
        out_specs=(
            P("dp", "seq", "tensor"),
            P(("dp", "seq"), "tensor"),
            P(("dp", "seq"), "tensor"),
            P(("dp", "seq"), "tensor"),
            P("tensor", ("dp", "seq")),
        ),
        check_vma=False,
    )
```
